32 devices in a mesh: groups: 2 (over x), dom: 16 (over z, y, core).
Axes of the slice: x: 2, y: 2, z: 4, core: 2. Of those that a mesh axis runs over, the one named last changes fastest.
Arguments:
- source: bfloat16 [72, 262144], P(None, ('groups', 'dom')), parts along dimension 1, may hold values from -6 to 6
- tile_weight: bfloat16 [8192, 128, 128], P('dom'), may hold values from -0.0625 to 0.0625
- tile_source: int32 [8192], P('dom'), may hold values from 0 to 127
- tile_slot: int32 [8192], P('dom'), may hold values from 0 to 15
- tile_count: int32 [16], P('dom'), may hold values from 64 to 512, as said below
- dest_block: int32 [256], P('dom'), may hold values from 0 to 63, as said below
- embed_weight: bfloat16 [1152, 1024], replicated, may hold values from -0.1875 to 0.1875
- embed_bias: float32 [1024], replicated, may hold values from -3 to 3
Outputs:
- remapped: bfloat16 [128, 72, 128], P(('groups', 'dom')), parts along dimension 0
- embedded: bfloat16 [1024, 1024], P(('groups', 'dom')), parts along dimension 0
The draws below stay inside these ranges and needn't reach their ends.
There are 2 independent parts, one for each index of `groups`. The reference program is written for one: setup_inputs(seed, part) draws one part's arguments, and reference() takes and returns one part's arrays. A program takes and returns all parts, laid end to end along the dimension named above; an argument that names none is the same for every part. Nothing has to cross between parts.
Inputs may be any that keep to these rules, and one draw needn't show every extreme that they name: `tile_count`: number of live tiles of each device; the later tile slots are unused. Some device has all 512 tiles live. `dest_block`: the owner of target block b is device b // 4. Within one device's 16 entries the blocks are distinct and at most 2 of them belong to any one owner; on every device some owner has exactly 2.
All inputs are finite; a program needn't handle non-finite values.
Results may differ from the reference program's by a relative error of at most 0.0046.
Values may be sent and summed in bfloat16 or wider, within the bound.
No kernel may reach another device: no remote copies, remote signals or barrier semaphores. Data moves between devices by JAX's collectives and lax.ppermute only.
A program may use at most 128 MiB of HBM per device.

```python
import jax
import jax.numpy as jnp
from jax import lax

CH = 72
EMB = 1024
BLK = 128
PATCH = 4
CAP = 2
SB_DEV = 64
TB_DEV = 4
TILES_DEV = 512
DSLOT = 16
HALO_B = 32
NSRC = 131072
NTB = 64
NPATCH = 512
N_DOM = 16


def draw_tile_count(key, part):
    levels_table = jnp.array([TILES_DEV, TILES_DEV // 2, TILES_DEV // 4, TILES_DEV // 8], dtype=jnp.int32)
    level_key, busiest_key = jax.random.split(key)
    levels = jax.random.randint(level_key, (N_DOM,), 0, 4)
    counts = levels_table[levels]
    busiest = jax.random.randint(busiest_key, (), 0, N_DOM)
    return jnp.where(jnp.arange(N_DOM) == busiest, TILES_DEV, counts).astype(jnp.int32)


def local_choice(sub_key):
    return jax.random.permutation(sub_key, TB_DEV)[:CAP]


def draw_dest_block(key, part):
    base_key = jax.random.fold_in(key, 11)
    device_keys = jax.random.split(base_key, N_DOM)
    owners_used = DSLOT // CAP

    def for_device(device_key):
        owner_key, local_key, order_key = jax.random.split(device_key, 3)
        owners = jax.random.permutation(owner_key, N_DOM)[:owners_used]
        chosen = jax.vmap(local_choice)(jax.random.split(local_key, owners_used))
        blocks = (owners[:, None] * TB_DEV + chosen).reshape(-1)
        return blocks[jax.random.permutation(order_key, DSLOT)]
    return jax.vmap(for_device)(device_keys).reshape(-1).astype(jnp.int32)


def set_ends(result, rng, least, top_value):
    longest = result.shape.index(max(result.shape))
    spots = []
    for shift in (0, 1):
        where = [jax.random.randint(jax.random.fold_in(rng, axis), (), 0, length) for axis, length in enumerate(result.shape)]
        where[longest] = (where[longest] + shift) % result.shape[longest]
        spots.append(tuple(where))
    return result.at[spots[0]].set(least).at[spots[1]].set(top_value)


def steps_of(stream_key, shape, pieces, least, high):
    loudness = 1.0
    for axis_at, shards_of in pieces:
        draws = jax.random.uniform(jax.random.fold_in(jax.random.fold_in(stream_key, 6), axis_at), (shards_of,), jnp.float32, least / len(pieces), high / len(pieces))
        loudness = loudness * jnp.repeat(jnp.exp(draws), shape[axis_at] // shards_of).reshape((-1,) + (1,) * (len(shape) - 1 - axis_at))
    return loudness


def scatter_about(stream_key, shape, width, reach, shards=(), kind=jnp.bfloat16):
    factor_of = steps_of(stream_key, shape, shards, -0.22, 0.18) if shards else 1.0
    entries = jax.random.normal(stream_key, shape, jnp.float32) * width * factor_of
    return jnp.minimum(jnp.maximum(entries, -reach), reach).astype(kind)


def setup_inputs(seed: int = 0, part: int = 0) -> dict:
    splits = jax.random.split(jax.random.key(seed), 9)
    part_splits = jax.random.split(jax.random.fold_in(splits[8], part), 9)
    return {
        "source": scatter_about(part_splits[0], (CH, NSRC), 1.0, 6.0, ((1, 16),)),
        "tile_weight": scatter_about(splits[1], (N_DOM * TILES_DEV, BLK, BLK), (TILES_DEV * BLK // (2 * TB_DEV)) ** -0.5, 0.0625, ((0, 16),)),
        "tile_source": set_ends(jax.random.randint(splits[2], (N_DOM * TILES_DEV,), 0, 2 * SB_DEV), jax.random.fold_in(splits[2], 1), 0, (2 * SB_DEV) - 1).astype(jnp.int32),
        "tile_slot": set_ends(jax.random.randint(splits[3], (N_DOM * TILES_DEV,), 0, DSLOT), jax.random.fold_in(splits[3], 1), 0, DSLOT - 1).astype(jnp.int32),
        "tile_count": draw_tile_count(jax.random.fold_in(splits[8], 71), part),
        "dest_block": draw_dest_block(jax.random.fold_in(splits[8], 71), part),
        "embed_weight": scatter_about(splits[6], (CH * PATCH * PATCH, EMB), (CH * PATCH * PATCH) ** -0.5, 0.1875),
        "embed_bias": scatter_about(splits[7], (EMB,), 0.5, 3.0, (), jnp.float32),
    }


def reference(source, tile_weight, tile_source, tile_slot, tile_count, dest_block, embed_weight, embed_bias):
    source_total = N_DOM * SB_DEV
    source_blocks = source.reshape(CH, source_total, BLK)

    def add_device(device, totals):
        device = jnp.asarray(device).astype(jnp.int32)
        first_tile = device * TILES_DEV
        offsets = lax.dynamic_slice_in_dim(tile_source, first_tile, TILES_DEV)
        global_ids = ((device * SB_DEV - HALO_B + offsets) % source_total).astype(jnp.int32)
        picked = jnp.take(source_blocks, global_ids, axis=1).astype(jnp.float32)
        weights = lax.dynamic_slice_in_dim(tile_weight, first_tile, TILES_DEV, 0).astype(jnp.float32)
        partial_sums = jnp.einsum("cti,tij->tcj", picked, weights, precision=lax.Precision.HIGHEST)
        active = jnp.arange(TILES_DEV, dtype=jnp.int32) < tile_count[device]
        partial_sums = jnp.where(active[:, None, None], partial_sums, jnp.zeros_like(partial_sums))
        slot_ids = lax.dynamic_slice_in_dim(tile_slot, first_tile, TILES_DEV)
        combined = jax.ops.segment_sum(partial_sums, slot_ids, num_segments=DSLOT)
        targets = lax.dynamic_slice_in_dim(dest_block, device * DSLOT, DSLOT)
        return totals.at[targets].add(combined)

    totals = lax.fori_loop(0, N_DOM, add_device, jnp.zeros((NTB, CH, BLK), jnp.float32))
    remapped = totals.astype(jnp.bfloat16)
    per_block = BLK // (PATCH * PATCH)
    patches = remapped.reshape(NTB, CH, PATCH, per_block, PATCH)
    patches = patches.transpose(0, 3, 1, 2, 4).reshape(NPATCH, CH * PATCH * PATCH)
    embedded = jnp.dot(patches, embed_weight, preferred_element_type=jnp.float32) + embed_bias
    return remapped, embedded.astype(jnp.bfloat16)
```

```python
import functools

import jax
import jax.numpy as jnp
from jax import lax
from jax.experimental import pallas as pl
from jax.experimental.pallas import tpu as pltpu
from jax.sharding import PartitionSpec as P

PATCH = 4
CAP = 2
TB_DEV = 4
SEG = 4
UNROLL = 4
CHUNK = 64
VMEM = pl.BlockSpec(memory_space=pltpu.VMEM)
SMEM = pl.BlockSpec(memory_space=pltpu.SMEM)
ANY = pl.BlockSpec(memory_space=pl.ANY)


def bits_of(tiles):
    return tiles.bit_length()


def list_sizes(tiles, slots):
    step = SEG * UNROLL
    entries = -(-(tiles + slots * (SEG - 1)) // step) * step
    return entries, entries // SEG


def schedule(tile_source, tile_slot, live_total, slots, own, rim):
    tiles = tile_source.shape[0]
    entries, segments = list_sizes(tiles, slots)
    ids = jnp.arange(tiles, dtype=jnp.int32)
    inner = (tile_source >= rim) & (tile_source < rim + own)
    kind = jnp.where(inner, 0, 1)
    block = jnp.where(inner | (tile_source < rim), tile_source - jnp.where(inner, rim, 0), tile_source - own)
    code = (block << bits_of(tiles)) | (tiles - ids)
    bins = jnp.where(ids < live_total, kind * slots + tile_slot, -1)
    chosen = bins[:, None] == jnp.arange(2 * slots, dtype=jnp.int32)[None, :]
    before = (ids[None, :] < ids[:, None]).astype(jnp.bfloat16)
    rank = jnp.dot(before, chosen.astype(jnp.bfloat16), preferred_element_type=jnp.float32)
    total = jnp.sum(chosen.astype(jnp.int32), axis=0)
    length = (total + SEG - 1) // SEG
    slot_ids = jnp.arange(slots, dtype=jnp.int32)
    length = length.reshape(2, slots)
    ends = jnp.sum(jnp.where(slot_ids[None, :] <= slot_ids[:, None], length[:, None, :], 0), axis=2)
    begins = (ends - length).reshape(-1)
    place = jnp.sum(jnp.where(chosen, rank.astype(jnp.int32) + begins[None, :] * SEG, 0), axis=1)
    place = jnp.where(bins >= 0, place + jnp.where(bins >= slots, entries, 0), -1)
    spots = jnp.arange(2 * entries, dtype=jnp.int32)
    listed = jnp.sum(jnp.where(place[None, :] == spots[:, None], code[None, :], 0), axis=1)
    segment_ids = jnp.arange(segments, dtype=jnp.int32)
    owner = jnp.sum((ends[:, None, :] <= segment_ids[None, :, None]).astype(jnp.int32), axis=2)
    owner = jnp.minimum(owner, slots - 1)
    return jnp.concatenate([listed, owner.reshape(-1), ends[:, slots - 1]])


def run_segments(kind, tiles, slots, meta, x, w, acc):
    entries, segments = list_sizes(tiles, slots)
    bits = bits_of(tiles)
    total = meta[2 * entries + 2 * segments + kind]

    def step(i, carry):
        results = []
        for u in range(UNROLL):
            first = kind * entries + (i * UNROLL + u) * SEG
            xs, ws = [], []
            for k in range(SEG):
                code = meta[first + k]
                column = pl.multiple_of((code >> bits) * 128, 128)
                xs.append(x[:, pl.ds(column, 128)])
                ws.append(w[tiles - (code & ((1 << bits) - 1))])
            results.append(
                jnp.dot(
                    jnp.concatenate(xs, axis=1),
                    jnp.concatenate(ws, axis=0),
                    preferred_element_type=jnp.float32,
                )
            )
        for u in range(UNROLL):
            slot = meta[2 * entries + kind * segments + i * UNROLL + u]
            acc[slot] += results[u]
        return carry

    lax.fori_loop(0, (total + UNROLL - 1) // UNROLL, step, 0)


def inner_kernel(tiles, slots, meta, count, source, weights, acc, held, sems):
    live = count[0]
    chunks = tiles // CHUNK

    def copy(c):
        part = pl.ds(c * CHUNK, CHUNK)
        return pltpu.make_async_copy(weights.at[part], held.at[part], sems.at[c])

    for c in range(chunks):
        pl.when(c * CHUNK < live)(lambda c=c: copy(c).start())
    acc[...] = jnp.zeros_like(acc)
    held[tiles] = jnp.zeros(held.shape[1:], held.dtype)
    for c in range(chunks):
        pl.when(c * CHUNK < live)(lambda c=c: copy(c).wait())
    run_segments(0, tiles, slots, meta, source, held, acc)


def halo_kernel(tiles, slots, meta, position, left, right, partial, held, out, x, acc, sems):
    rim = left.shape[1]
    copies = [
        pltpu.make_async_copy(left, x.at[:, pl.ds(0, rim)], sems.at[0]),
        pltpu.make_async_copy(right, x.at[:, pl.ds(rim, rim)], sems.at[1]),
    ]
    for c in copies:
        c.start()
    out[...] = jnp.zeros_like(out)
    acc[...] = partial[...]
    for c in copies:
        c.wait()
    run_segments(1, tiles, slots, meta, x, held, acc)

    def place(s, carry):
        out[position[s]] = acc[s].astype(out.dtype)
        return carry

    lax.fori_loop(0, slots, place, 0)


def final_kernel(labels, incoming, choose, weight, bias, remapped, embedded, acc, turned):
    acc[...] = jnp.zeros_like(acc)

    def add(r, carry):
        label = labels[r]

        @pl.when(label >= 0)
        def _():
            acc[label] += incoming[r].astype(jnp.float32)

        return carry

    lax.fori_loop(0, incoming.shape[0], add, 0)
    embed(acc, choose, weight, bias, remapped, embedded, turned)


def embed(acc, choose, weight, bias, remapped, embedded, turned):
    blocks, channels, cells = acc.shape
    for b in range(blocks):
        value = acc[b].astype(jnp.bfloat16)
        remapped[b] = value
        turned[b] = lax.dot_general(
            choose[...], value, (((1,), (1,)), ((), ())), preferred_element_type=jnp.float32
        )
    per_block = cells // (PATCH * PATCH)
    total = jnp.broadcast_to(bias[...], (blocks * per_block, bias.shape[1]))
    for s in range(PATCH * PATCH):
        rows = turned[:, s * per_block : (s + 1) * per_block, :]
        rows = rows.reshape(blocks * per_block, channels).astype(jnp.bfloat16)
        total = total + jnp.dot(rows, weight[s], preferred_element_type=jnp.float32)
    embedded[...] = total.astype(jnp.bfloat16)


def chooser(cells):
    per_block = cells // (PATCH * PATCH)
    row = jnp.arange(cells, dtype=jnp.int32)
    r, q, p = row // (PATCH * per_block), row // per_block % PATCH, row % per_block
    wanted = r * (PATCH * per_block) + p * PATCH + q
    return (wanted[:, None] == jnp.arange(cells, dtype=jnp.int32)[None, :]).astype(jnp.bfloat16)


def local(
    source, tile_weight, tile_source, tile_slot, tile_count, dest_block, embed_weight, embed_bias
):
    channels, own_cells = source.shape
    tiles, block_size, _ = tile_weight.shape
    own = own_cells // block_size
    rim = own // 2
    slots = dest_block.shape[0]
    peers = lax.axis_size("dom")
    width = rim * block_size
    emb = embed_weight.shape[1]

    head = lax.slice_in_dim(source, 0, width, axis=1)
    tail = lax.slice_in_dim(source, own_cells - width, own_cells, axis=1)
    left = lax.ppermute(tail, "dom", [(i, (i + 1) % peers) for i in range(peers)])
    right = lax.ppermute(head, "dom", [((i + 1) % peers, i) for i in range(peers)])

    meta = schedule(tile_source, tile_slot, tile_count[0], slots, own, rim)
    slot_ids = jnp.arange(slots, dtype=jnp.int32)
    owners = dest_block // TB_DEV
    earlier = (owners[None, :] == owners[:, None]) & (slot_ids[None, :] < slot_ids[:, None])
    position = owners * CAP + jnp.sum(earlier.astype(jnp.int32), axis=1)
    rows = jnp.arange(peers * CAP, dtype=jnp.int32)
    placing = position[None, :] == rows[:, None]
    labels = jnp.sum(jnp.where(placing, (dest_block % TB_DEV)[None, :] + 1, 0), axis=1) - 1
    arrived = lax.all_to_all(labels, "dom", split_axis=0, concat_axis=0, tiled=True)

    acc_shape = (slots, channels, block_size)
    held_shape = (tiles + 1, block_size, block_size)
    partial, held = pl.pallas_call(
        functools.partial(inner_kernel, tiles, slots),
        out_shape=(
            pltpu.VMEM(acc_shape, jnp.float32),
            pltpu.VMEM(held_shape, jnp.bfloat16),
        ),
        in_specs=[SMEM, SMEM, VMEM, ANY],
        out_specs=(VMEM, VMEM),
        scratch_shapes=[pltpu.SemaphoreType.DMA((tiles // CHUNK,))],
        compiler_params=pltpu.CompilerParams(vmem_limit_bytes=8 << 20),
        cost_estimate=pl.CostEstimate(
            flops=tiles * channels * block_size * block_size,
            bytes_accessed=tile_weight.size * 2,
            transcendentals=0,
        ),
        name="inner_tiles",
    )(meta, tile_count, source, pltpu.with_memory_space_constraint(tile_weight, pltpu.HBM))

    outgoing = pl.pallas_call(
        functools.partial(halo_kernel, tiles, slots),
        out_shape=jax.ShapeDtypeStruct((peers * CAP, channels, block_size), jnp.bfloat16),
        in_specs=[SMEM, SMEM, ANY, ANY, VMEM, VMEM],
        out_specs=VMEM,
        scratch_shapes=[
            pltpu.VMEM((channels, 2 * width), jnp.bfloat16),
            pltpu.VMEM(acc_shape, jnp.float32),
            pltpu.SemaphoreType.DMA((2,)),
        ],
        compiler_params=pltpu.CompilerParams(vmem_limit_bytes=16 << 20),
        cost_estimate=pl.CostEstimate(
            flops=tiles * channels * block_size * block_size,
            bytes_accessed=4 * channels * width * 2,
            transcendentals=0,
        ),
        name="halo_tiles",
    )(
        meta,
        position,
        left,
        right,
        pltpu.with_memory_space_constraint(partial, pltpu.VMEM),
        pltpu.with_memory_space_constraint(held, pltpu.VMEM),
    )

    incoming = lax.all_to_all(outgoing, "dom", split_axis=0, concat_axis=0, tiled=True)

    area = PATCH * PATCH
    weight = embed_weight.reshape(channels, area, emb).transpose(1, 0, 2)
    per_block = block_size // area
    return pl.pallas_call(
        final_kernel,
        out_shape=(
            jax.ShapeDtypeStruct((TB_DEV, channels, block_size), jnp.bfloat16),
            jax.ShapeDtypeStruct((TB_DEV * per_block, emb), jnp.bfloat16),
        ),
        in_specs=[SMEM, VMEM, VMEM, VMEM, VMEM],
        out_specs=(VMEM, VMEM),
        scratch_shapes=[
            pltpu.VMEM((TB_DEV, channels, block_size), jnp.float32),
            pltpu.VMEM((TB_DEV, block_size, channels), jnp.float32),
        ],
        compiler_params=pltpu.CompilerParams(vmem_limit_bytes=16 << 20),
        name="embed",
    )(arrived, incoming, chooser(block_size), weight, embed_bias.reshape(1, emb))


def solution(mesh):
    placed = (
        P(None, ("groups", "dom")),
        P("dom", None, None),
        P("dom"),
        P("dom"),
        P("dom"),
        P("dom"),
        P(),
        P(),
    )
    return jax.shard_map(
        local,
        mesh=mesh,
        in_specs=placed,
        out_specs=(P(("groups", "dom"), None, None), P(("groups", "dom"), None)),
        check_vma=False,
    )
```

```python
import functools

import jax
import jax.numpy as jnp
from jax import lax
from jax.experimental import pallas as pl
from jax.experimental.pallas import tpu as pltpu
from jax.sharding import PartitionSpec as P

PATCH = 4
CAP = 2
TB_DEV = 4
LANES = 128
SEG = 4
UNROLL = 4
CHUNK = 64
VMEM = pl.BlockSpec(memory_space=pltpu.VMEM)
SMEM = pl.BlockSpec(memory_space=pltpu.SMEM)
ANY = pl.BlockSpec(memory_space=pl.ANY)


def list_rows(tiles, slots):
    entries = -(-(tiles + slots * (SEG - 1)) // LANES)
    segments = -(-entries // SEG)
    return entries, segments, -(-(2 * (entries + segments) + 1) // 8) * 8


def iota(shape, dim):
    return lax.broadcasted_iota(jnp.int32, shape, dim)


def schedule(source, slot, live, core, slots, own, rim, out):
    tiles = source.shape[1]
    bits = tiles.bit_length()
    entries, segments, rows = list_rows(tiles, slots)
    ids = iota((1, tiles), 1)
    on_left, on_right = source < rim, source >= rim + own
    inner = ~(on_left | on_right)
    near = (on_left & (core == 1)) | (on_right & (core == 0))
    offset = jnp.where(on_right, source - own - rim, source)
    block = jnp.where(inner, source - rim, jnp.where(near, own + offset, offset))
    late = ~(inner | near)
    bins = jnp.where(ids < live, slot + jnp.where(late, slots, 0), -1)
    chosen = bins == iota((2 * slots, tiles), 0)
    ones = jnp.where(chosen, 1.0, 0.0)
    before = jnp.where(iota((tiles, tiles), 0) < iota((tiles, tiles), 1), 1.0, 0.0)
    rank = jnp.dot(
        ones.astype(jnp.bfloat16), before.astype(jnp.bfloat16), preferred_element_type=jnp.float32
    )
    total = jnp.sum(ones, axis=1, keepdims=True).astype(jnp.int32)
    length = jnp.broadcast_to((total + (SEG - 1)) // SEG, (2 * slots, LANES))
    a, b = iota((2 * slots, 2 * slots), 0), iota((2 * slots, 2 * slots), 1)
    upto = jnp.where((b <= a) & ((b >= slots) == (a >= slots)), 1.0, 0.0)
    ends = jnp.dot(
        upto.astype(jnp.bfloat16),
        length.astype(jnp.float32).astype(jnp.bfloat16),
        preferred_element_type=jnp.float32,
    ).astype(jnp.int32)
    begins = (ends - length)[:, :1].astype(jnp.float32)
    place = jnp.sum(jnp.where(chosen, rank + begins * SEG, 0.0), axis=0, keepdims=True)
    place = place.astype(jnp.int32) + jnp.where(late, entries * LANES, 0)
    place = jnp.where(bins >= 0, place, -1)
    count = tiles - ids
    at_row = (place >> 7) == iota((rows, tiles), 0)
    at_lane = jnp.where((place & (LANES - 1)) == iota((LANES, tiles), 0), 1.0, 0.0)

    def listed(value):
        return lax.dot_general(
            jnp.where(at_row, value.astype(jnp.float32), 0.0).astype(jnp.bfloat16),
            at_lane.astype(jnp.bfloat16),
            (((1,), (1,)), ((), ())),
            preferred_element_type=jnp.float32,
        ).astype(jnp.int32)

    out[...] = (listed(block) << bits) | (listed(count >> 5) << 5) | listed(count & 31)
    for k in range(2):
        mine = ends[k * slots : (k + 1) * slots, :]
        for r in range(segments):
            passed = jnp.where(mine <= iota((slots, LANES), 1) + r * LANES, 1.0, 0.0)
            owner = jnp.sum(passed, axis=0, keepdims=True).astype(jnp.int32)
            spot = 2 * entries + k * segments + r
            out[spot : spot + 1, :] = jnp.minimum(owner, slots - 1)
    spot = 2 * (entries + segments)
    out[spot : spot + 1, :] = jnp.where(
        iota((1, LANES), 1) == 0, ends[slots - 1 : slots, :], ends[2 * slots - 1 : 2 * slots, :]
    )


def run_segments(kind, tiles, slots, meta, x, w, acc):
    entries, segments, _ = list_rows(tiles, slots)
    bits = tiles.bit_length()
    total = meta[2 * (entries + segments), kind]

    def step(i, carry):
        results = []
        for u in range(UNROLL):
            first = (i * UNROLL + u) * SEG
            row, lane = kind * entries + (first >> 7), first & (LANES - 1)
            xs, ws = [], []
            for k in range(SEG):
                code = meta[row, lane + k]
                column = pl.multiple_of((code >> bits) * LANES, LANES)
                xs.append(x[:, pl.ds(column, LANES)])
                ws.append(w[tiles - (code & ((1 << bits) - 1))])
            results.append(
                jnp.dot(
                    jnp.concatenate(xs, axis=1),
                    jnp.concatenate(ws, axis=0),
                    preferred_element_type=jnp.float32,
                )
            )
        for u in range(UNROLL):
            g = i * UNROLL + u
            slot = meta[2 * entries + kind * segments + (g >> 7), g & (LANES - 1)]
            acc[slot] += results[u]
        return carry

    lax.fori_loop(0, (total + UNROLL - 1) // UNROLL, step, 0)


def early_kernel(
    slots, core, count, tile_source, tile_slot, source, near, weights, acc, held, lists, x, meta, sems
):
    tiles = tile_source.shape[1]
    cells = source.shape[1]
    live = count[0]
    chunks = tiles // CHUNK

    def copy(c):
        part = pl.ds(c * CHUNK, CHUNK)
        return pltpu.make_async_copy(weights.at[part], held.at[part], sems.at[c])

    cells_in = [
        pltpu.make_async_copy(source, x.at[:, pl.ds(0, cells)], sems.at[chunks]),
        pltpu.make_async_copy(near, x.at[:, pl.ds(cells, near.shape[1])], sems.at[chunks + 1]),
    ]
    for c in cells_in:
        c.start()
    for c in range(chunks):
        pl.when(c * CHUNK < live)(lambda c=c: copy(c).start())
    own = cells // LANES
    schedule(tile_source[...], tile_slot[...], live, core[0], slots, own, own // 2, lists)
    to_scalars = pltpu.make_async_copy(lists, meta, sems.at[chunks + 2])
    to_scalars.start()
    acc[...] = jnp.zeros_like(acc)
    held[tiles] = jnp.zeros(held.shape[1:], held.dtype)
    to_scalars.wait()
    for c in cells_in:
        c.wait()
    for c in range(chunks):
        pl.when(c * CHUNK < live)(lambda c=c: copy(c).wait())
    run_segments(0, tiles, slots, meta, x, held, acc)


def late_kernel(tiles, slots, meta, place, far, partial, held, *rest):
    *outs, acc = rest
    acc[...] = partial[...]
    for out in outs:
        out[...] = jnp.zeros_like(out)
    run_segments(1, tiles, slots, meta, far, held, acc)

    def put(s, carry):
        code = place[s]
        for q, out in enumerate(outs):

            @pl.when((code >> 16) == q)
            def _(out=out):
                out[code & 0xFFFF] = acc[s].astype(out.dtype)

        return carry

    lax.fori_loop(0, slots, put, 0)


def plane_kernel(planes, me, *refs):
    members = len([r for r in refs if len(r.shape) == 1]) + 1
    labels, (own, *rows), rest = refs[: members - 1], refs[members - 1 : 2 * members - 1], refs[2 * members - 1 :]
    *outs, total = rest
    total[...] = own[...]
    for label, row in zip(labels, rows):
        for r in range(row.shape[0]):
            spot = label[r]

            @pl.when(spot >= 0)
            def _(r=r, row=row, spot=spot):
                total[(r // CAP) * TB_DEV + spot] += row[r].astype(jnp.float32)

    if len(outs) == 1:
        outs[0][...] = total[...].astype(outs[0].dtype)
    else:
        for m, out in enumerate(outs):
            out[...] = total[pl.ds((me[0] ^ m) * TB_DEV, TB_DEV)].astype(out.dtype)


def final_kernel(choose, weight, bias, *refs):
    *parts, remapped, embedded, turned = refs
    blocks, channels, cells = remapped.shape
    for b in range(blocks):
        value = sum(p[i + b].astype(jnp.float32) for p in parts for i in range(0, p.shape[0], blocks))
        value = value.astype(jnp.bfloat16)
        remapped[b] = value
        turned[b] = lax.dot_general(
            choose[...], value, (((1,), (1,)), ((), ())), preferred_element_type=jnp.float32
        )
    per_block = cells // (PATCH * PATCH)
    total = jnp.broadcast_to(bias[...], (blocks * per_block, bias.shape[1]))
    for s in range(PATCH * PATCH):
        rows = turned[:, s * per_block : (s + 1) * per_block, :]
        rows = rows.reshape(blocks * per_block, channels).astype(jnp.bfloat16)
        total = total + jnp.dot(rows, weight[s], preferred_element_type=jnp.float32)
    embedded[...] = total.astype(jnp.bfloat16)


def chooser(cells):
    per_block = cells // (PATCH * PATCH)
    row = jnp.arange(cells, dtype=jnp.int32)
    r, q, p = row // (PATCH * per_block), row // per_block % PATCH, row % per_block
    wanted = r * (PATCH * per_block) + p * PATCH + q
    return (wanted[:, None] == jnp.arange(cells, dtype=jnp.int32)[None, :]).astype(jnp.bfloat16)


def in_vmem(x):
    return pltpu.with_memory_space_constraint(x, pltpu.VMEM)


def limit(mib):
    return pltpu.CompilerParams(vmem_limit_bytes=mib << 20)


def local(
    source, tile_weight, tile_source, tile_slot, tile_count, dest_block, embed_weight, embed_bias
):
    channels, own_cells = source.shape
    tiles, block_size, _ = tile_weight.shape
    slots = dest_block.shape[0]
    peers = lax.axis_size("dom")
    me = lax.axis_index("dom").astype(jnp.int32)
    core = me % 2
    width = own_cells // 2
    emb = embed_weight.shape[1]
    members = 4 if peers == 16 else 2
    planes = peers // members

    def swap(x, q):
        return lax.ppermute(x, "dom", [(i, i ^ q) for i in range(peers)])

    far_out = lax.dynamic_slice_in_dim(source, core * width, width, axis=1)
    far = lax.ppermute(
        far_out, "dom", [(i, (i + (1 if i % 2 else -1)) % peers) for i in range(peers)]
    )
    near_out = lax.dynamic_slice_in_dim(source, (1 - core) * width, width, axis=1)
    near = swap(near_out, 1)

    slot_ids = jnp.arange(slots, dtype=jnp.int32)
    owners = dest_block // TB_DEV
    earlier = (owners[None, :] == owners[:, None]) & (slot_ids[None, :] < slot_ids[:, None])
    row = owners // members * CAP + jnp.sum(earlier.astype(jnp.int32), axis=1)
    member = (owners % members) ^ (me % members)
    block_row = dest_block % TB_DEV
    place = jnp.where(member == 0, owners // members * TB_DEV + block_row, (member << 16) | row)
    row_total = planes * CAP
    spots = jnp.arange(members * row_total, dtype=jnp.int32)
    taken = (member * row_total + row)[None, :] == spots[:, None]
    labels = jnp.sum(jnp.where(taken, block_row[None, :] + 1, 0), axis=1) - 1
    labels = [swap(labels[q * row_total : (q + 1) * row_total], q) for q in range(1, members)]

    acc_shape = (slots, channels, block_size)
    held_shape = (tiles + 1, block_size, block_size)
    _, _, list_total = list_rows(tiles, slots)
    chunks = tiles // CHUNK
    partial, held, lists = pl.pallas_call(
        functools.partial(early_kernel, slots),
        out_shape=(
            pltpu.VMEM(acc_shape, jnp.float32),
            pltpu.VMEM(held_shape, jnp.bfloat16),
            jax.ShapeDtypeStruct((list_total, LANES), jnp.int32),
        ),
        in_specs=[SMEM, SMEM, VMEM, VMEM, ANY, ANY, ANY],
        out_specs=(VMEM, VMEM, VMEM),
        scratch_shapes=[
            pltpu.VMEM((channels, own_cells + width), jnp.bfloat16),
            pltpu.SMEM((list_total, LANES), jnp.int32),
            pltpu.SemaphoreType.DMA((chunks + 3,)),
        ],
        compiler_params=limit(12),
        cost_estimate=pl.CostEstimate(
            flops=tiles * channels * block_size * block_size,
            bytes_accessed=tile_weight.size * 2,
            transcendentals=0,
        ),
        name="early_tiles",
    )(
        core[None],
        tile_count,
        tile_source[None, :],
        tile_slot[None, :],
        source,
        near,
        pltpu.with_memory_space_constraint(tile_weight, pltpu.HBM),
    )

    own_shape = pltpu.VMEM((planes * TB_DEV, channels, block_size), jnp.float32)
    row_shape = jax.ShapeDtypeStruct((row_total, channels, block_size), jnp.bfloat16)
    own, *rows = pl.pallas_call(
        functools.partial(late_kernel, tiles, slots),
        out_shape=(own_shape,) + (row_shape,) * (members - 1),
        in_specs=[SMEM, SMEM, VMEM, VMEM, VMEM],
        out_specs=(VMEM,) * members,
        scratch_shapes=[pltpu.VMEM(acc_shape, jnp.float32)],
        compiler_params=limit(12),
        cost_estimate=pl.CostEstimate(
            flops=tiles * channels * block_size * block_size,
            bytes_accessed=2 * channels * width * 2,
            transcendentals=0,
        ),
        name="late_tiles",
    )(lists, place, far, in_vmem(partial), in_vmem(held))

    rows = [swap(r, q + 1) for q, r in enumerate(rows)]
    part = (TB_DEV, channels, block_size)
    by_swap = planes <= 4
    if by_swap:
        part_shapes = (pltpu.VMEM(part, jnp.float32),)
        part_shapes += (jax.ShapeDtypeStruct(part, jnp.bfloat16),) * (planes - 1)
    else:
        part_shapes = (jax.ShapeDtypeStruct((planes * TB_DEV,) + part[1:], jnp.bfloat16),)
    parts = pl.pallas_call(
        functools.partial(plane_kernel, planes),
        out_shape=part_shapes,
        in_specs=[SMEM] * members + [VMEM] * members,
        out_specs=(VMEM,) * len(part_shapes),
        scratch_shapes=[pltpu.VMEM(own_shape.shape, jnp.float32)],
        compiler_params=limit(24),
        name="plane_sum",
    )((me // members)[None], *labels, in_vmem(own), *rows)
    if by_swap:
        parts = [parts[0]] + [swap(p, (m + 1) * members) for m, p in enumerate(parts[1:])]
    else:
        columns = [[z * members + i for z in range(planes)] for i in range(members)]
        parts = [lax.all_to_all(parts[0], "dom", 0, 0, tiled=True, axis_index_groups=columns)]

    area = PATCH * PATCH
    weight = embed_weight.reshape(channels, area, emb).transpose(1, 0, 2)
    per_block = block_size // area
    return pl.pallas_call(
        final_kernel,
        out_shape=(
            jax.ShapeDtypeStruct(part, jnp.bfloat16),
            jax.ShapeDtypeStruct((TB_DEV * per_block, emb), jnp.bfloat16),
        ),
        in_specs=[VMEM] * (3 + len(parts)),
        out_specs=(VMEM, VMEM),
        scratch_shapes=[pltpu.VMEM((TB_DEV, block_size, channels), jnp.float32)],
        compiler_params=limit(16),
        name="embed",
    )(chooser(block_size), weight, embed_bias.reshape(1, emb), *parts)


def solution(mesh):
    placed = (
        P(None, ("groups", "dom")),
        P("dom", None, None),
        P("dom"),
        P("dom"),
        P("dom"),
        P("dom"),
        P(),
        P(),
    )
    return jax.shard_map(
        local,
        mesh=mesh,
        in_specs=placed,
        out_specs=(P(("groups", "dom"), None, None), P(("groups", "dom"), None)),
        check_vma=False,
    )
```

```python
import functools

import jax
import jax.numpy as jnp
from jax import lax
from jax.experimental import pallas as pl
from jax.experimental.pallas import tpu as pltpu
from jax.sharding import PartitionSpec as P

PATCH = 4
CAP = 2
TB_DEV = 4
LANES = 128
SEG = 4
EARLY_UNROLL = 16
LATE_UNROLL = 8
CHUNK = 64
VMEM = pl.BlockSpec(memory_space=pltpu.VMEM)
SMEM = pl.BlockSpec(memory_space=pltpu.SMEM)
ANY = pl.BlockSpec(memory_space=pl.ANY)


def list_rows(tiles, slots):
    step = SEG * EARLY_UNROLL
    entries = -(-(-(-(tiles + slots * (SEG - 1)) // step) * step) // LANES)
    segments = -(-entries // SEG)
    return entries, segments, -(-(2 * (entries + segments) + 1) // 8) * 8


def iota(shape, dim):
    return lax.broadcasted_iota(jnp.int32, shape, dim)


def schedule(source, slot, live, core, slots, own, rim, out):
    tiles = source.shape[1]
    bits = tiles.bit_length()
    entries, segments, rows = list_rows(tiles, slots)
    ids = iota((1, tiles), 1)
    on_left, on_right = source < rim, source >= rim + own
    inner = ~(on_left | on_right)
    near = (on_left & (core == 1)) | (on_right & (core == 0))
    offset = jnp.where(on_right, source - own - rim, source)
    block = jnp.where(inner, source - rim, jnp.where(near, own + offset, offset))
    late = ~(inner | near)
    bins = jnp.where(ids < live, slot + jnp.where(late, slots, 0), -1)
    chosen = bins == iota((2 * slots, tiles), 0)
    ones = jnp.where(chosen, 1.0, 0.0)
    before = jnp.where(iota((tiles, tiles), 0) < iota((tiles, tiles), 1), 1.0, 0.0)
    rank = jnp.dot(
        ones.astype(jnp.bfloat16), before.astype(jnp.bfloat16), preferred_element_type=jnp.float32
    )
    total = jnp.sum(ones, axis=1, keepdims=True).astype(jnp.int32)
    length = jnp.broadcast_to((total + (SEG - 1)) // SEG, (2 * slots, LANES))
    a, b = iota((2 * slots, 2 * slots), 0), iota((2 * slots, 2 * slots), 1)
    upto = jnp.where((b <= a) & ((b >= slots) == (a >= slots)), 1.0, 0.0)
    ends = jnp.dot(
        upto.astype(jnp.bfloat16),
        length.astype(jnp.float32).astype(jnp.bfloat16),
        preferred_element_type=jnp.float32,
    ).astype(jnp.int32)
    begins = (ends - length)[:, :1].astype(jnp.float32)
    place = jnp.sum(jnp.where(chosen, rank + begins * SEG, 0.0), axis=0, keepdims=True)
    place = place.astype(jnp.int32) + jnp.where(late, entries * LANES, 0)
    place = jnp.where(bins >= 0, place, -1)
    count = tiles - ids
    at_row = (place >> 7) == iota((rows, tiles), 0)
    at_lane = jnp.where((place & (LANES - 1)) == iota((LANES, tiles), 0), 1.0, 0.0)

    def listed(value):
        return lax.dot_general(
            jnp.where(at_row, value.astype(jnp.float32), 0.0).astype(jnp.bfloat16),
            at_lane.astype(jnp.bfloat16),
            (((1,), (1,)), ((), ())),
            preferred_element_type=jnp.float32,
        ).astype(jnp.int32)

    out[...] = (listed(block) << bits) | (listed(count >> 5) << 5) | listed(count & 31)
    for k in range(2):
        mine = ends[k * slots : (k + 1) * slots, :]
        for r in range(segments):
            passed = jnp.where(mine <= iota((slots, LANES), 1) + r * LANES, 1.0, 0.0)
            owner = jnp.sum(passed, axis=0, keepdims=True).astype(jnp.int32)
            spot = 2 * entries + k * segments + r
            out[spot : spot + 1, :] = jnp.minimum(owner, slots - 1)
    spot = 2 * (entries + segments)
    out[spot : spot + 1, :] = jnp.where(
        iota((1, LANES), 1) == 0, ends[slots - 1 : slots, :], ends[2 * slots - 1 : 2 * slots, :]
    )


def run_segments(kind, unroll, tiles, slots, meta, x, w, acc):
    entries, segments, _ = list_rows(tiles, slots)
    bits = tiles.bit_length()
    total = meta[2 * (entries + segments), kind]

    def step(i, carry):
        results = []
        for u in range(unroll):
            first = (i * unroll + u) * SEG
            row, lane = kind * entries + (first >> 7), first & (LANES - 1)
            xs, ws = [], []
            for k in range(SEG):
                code = meta[row, lane + k]
                column = pl.multiple_of((code >> bits) * LANES, LANES)
                xs.append(x[:, pl.ds(column, LANES)])
                ws.append(w[tiles - (code & ((1 << bits) - 1))])
            results.append(
                jnp.dot(
                    jnp.concatenate(xs, axis=1),
                    jnp.concatenate(ws, axis=0),
                    preferred_element_type=jnp.float32,
                )
            )
        for u in range(unroll):
            g = i * unroll + u
            slot = meta[2 * entries + kind * segments + (g >> 7), g & (LANES - 1)]
            acc[slot] += results[u]
        return carry

    lax.fori_loop(0, (total + unroll - 1) // unroll, step, 0)


def early_kernel(
    slots, core, count, tile_source, tile_slot, source, near, weights, acc, held, lists, x, ids, meta, sems
):
    tiles = tile_source.shape[1]
    cells = source.shape[1]
    live = count[0]
    chunks = tiles // CHUNK

    def copy(c):
        part = pl.ds(c * CHUNK, CHUNK)
        return pltpu.make_async_copy(weights.at[part], held.at[part], sems.at[c])

    ids_in = [
        pltpu.make_async_copy(tile_source, ids.at[0], sems.at[chunks + 3]),
        pltpu.make_async_copy(tile_slot, ids.at[1], sems.at[chunks + 4]),
    ]
    for c in ids_in:
        c.start()
    for c in range(chunks):
        pl.when(c * CHUNK < live)(lambda c=c: copy(c).start())
    half = cells // 2
    first = pl.multiple_of(core[0] * half, LANES)
    cells_in = [
        pltpu.make_async_copy(source, x.at[:, pl.ds(0, cells)], sems.at[chunks]),
        pltpu.make_async_copy(
            near.at[:, pl.ds(first, half)], x.at[:, pl.ds(cells, half)], sems.at[chunks + 1]
        ),
    ]
    for c in cells_in:
        c.start()
    own = cells // LANES
    for c in ids_in:
        c.wait()
    schedule(ids[0], ids[1], live, core[0], slots, own, own // 2, lists)
    to_scalars = pltpu.make_async_copy(lists, meta, sems.at[chunks + 2])
    to_scalars.start()
    acc[...] = jnp.zeros_like(acc)
    held[tiles] = jnp.zeros(held.shape[1:], held.dtype)
    to_scalars.wait()
    for c in cells_in:
        c.wait()
    for c in range(chunks):
        pl.when(c * CHUNK < live)(lambda c=c: copy(c).wait())
    run_segments(0, EARLY_UNROLL, tiles, slots, meta, x, held, acc)


def late_kernel(tiles, slots, meta, place, far, partial, held, *rest):
    *outs, acc = rest
    acc[...] = partial[...]
    for out in outs:
        out[...] = jnp.zeros_like(out)
    run_segments(1, LATE_UNROLL, tiles, slots, meta, far, held, acc)

    def put(s, carry):
        code = place[s]
        for q, out in enumerate(outs):

            @pl.when((code >> 16) == q)
            def _(out=out):
                out[code & 0xFFFF] = acc[s].astype(out.dtype)

        return carry

    lax.fori_loop(0, slots, put, 0)


def plane_kernel(planes, me, *refs):
    members = len([r for r in refs if len(r.shape) == 1]) + 1
    labels, (own, *rows), rest = refs[: members - 1], refs[members - 1 : 2 * members - 1], refs[2 * members - 1 :]
    *outs, total = rest
    total[...] = own[...]
    for label, row in zip(labels, rows):
        for r in range(row.shape[0]):
            spot = label[r]

            @pl.when(spot >= 0)
            def _(r=r, row=row, spot=spot):
                total[(r // CAP) * TB_DEV + spot] += row[r].astype(jnp.float32)

    if len(outs) == 1:
        outs[0][...] = total[...].astype(outs[0].dtype)
    else:
        for m, out in enumerate(outs):
            out[...] = total[pl.ds((me[0] ^ m) * TB_DEV, TB_DEV)].astype(out.dtype)


def final_kernel(choose, weight, bias, *refs):
    *parts, remapped, embedded, turned = refs
    blocks, channels, cells = remapped.shape
    for b in range(blocks):
        value = sum(p[i + b].astype(jnp.float32) for p in parts for i in range(0, p.shape[0], blocks))
        value = value.astype(jnp.bfloat16)
        remapped[b] = value
        turned[b] = lax.dot_general(
            choose[...], value, (((1,), (1,)), ((), ())), preferred_element_type=jnp.float32
        )
    per_block = cells // (PATCH * PATCH)
    total = jnp.broadcast_to(bias[...], (blocks * per_block, bias.shape[1]))
    for s in range(PATCH * PATCH):
        rows = turned[:, s * per_block : (s + 1) * per_block, :]
        rows = rows.reshape(blocks * per_block, channels).astype(jnp.bfloat16)
        total = total + jnp.dot(rows, weight[s], preferred_element_type=jnp.float32)
    embedded[...] = total.astype(jnp.bfloat16)


def chooser(cells):
    per_block = cells // (PATCH * PATCH)
    row = jnp.arange(cells, dtype=jnp.int32)
    r, q, p = row // (PATCH * per_block), row // per_block % PATCH, row % per_block
    wanted = r * (PATCH * per_block) + p * PATCH + q
    return (wanted[:, None] == jnp.arange(cells, dtype=jnp.int32)[None, :]).astype(jnp.bfloat16)


def in_vmem(x):
    return pltpu.with_memory_space_constraint(x, pltpu.VMEM)


def in_hbm(x):
    return pltpu.with_memory_space_constraint(x, pltpu.HBM)


def limit(mib):
    return pltpu.CompilerParams(vmem_limit_bytes=mib << 20)


def local(
    source, tile_weight, tile_source, tile_slot, tile_count, dest_block, embed_weight, embed_bias
):
    channels, own_cells = source.shape
    tiles, block_size, _ = tile_weight.shape
    slots = dest_block.shape[0]
    peers = lax.axis_size("dom")
    me = lax.axis_index("dom").astype(jnp.int32)
    core = me & 1
    width = own_cells // 2
    emb = embed_weight.shape[1]
    members = 4 if peers == 16 else 2
    planes = peers // members

    def swap(x, q):
        return lax.ppermute(x, "dom", [(i, i ^ q) for i in range(peers)])

    near = swap(source, 1)
    far = lax.ppermute(
        lax.dynamic_slice_in_dim(source, core * width, width, axis=1),
        "dom",
        [(i, (i + (1 if i % 2 else -1)) % peers) for i in range(peers)],
    )

    acc_shape = (slots, channels, block_size)
    _, _, list_total = list_rows(tiles, slots)
    partial, held, lists = pl.pallas_call(
        functools.partial(early_kernel, slots),
        out_shape=(
            pltpu.VMEM(acc_shape, jnp.float32),
            pltpu.VMEM((tiles + 1, block_size, block_size), jnp.bfloat16),
            jax.ShapeDtypeStruct((list_total, LANES), jnp.int32),
        ),
        in_specs=[SMEM, SMEM, ANY, ANY, ANY, ANY, ANY],
        out_specs=(VMEM, VMEM, VMEM),
        scratch_shapes=[
            pltpu.VMEM((channels, own_cells + width), jnp.bfloat16),
            pltpu.VMEM((2, 1, tiles), jnp.int32),
            pltpu.SMEM((list_total, LANES), jnp.int32),
            pltpu.SemaphoreType.DMA((tiles // CHUNK + 5,)),
        ],
        compiler_params=limit(12),
        cost_estimate=pl.CostEstimate(
            flops=tiles * channels * block_size * block_size,
            bytes_accessed=tile_weight.size * 2,
            transcendentals=0,
        ),
        name="early_tiles",
    )(
        core[None],
        tile_count,
        in_hbm(tile_source[None, :]),
        in_hbm(tile_slot[None, :]),
        in_hbm(source),
        near,
        in_hbm(tile_weight),
    )

    lists, dest_block, embed_weight = lax.optimization_barrier((lists, dest_block, embed_weight))
    slot_ids = jnp.arange(slots, dtype=jnp.int32)
    owners = dest_block // TB_DEV
    earlier = (owners[None, :] == owners[:, None]) & (slot_ids[None, :] < slot_ids[:, None])
    row = owners // members * CAP + jnp.sum(earlier.astype(jnp.int32), axis=1)
    member = (owners % members) ^ (me & (members - 1))
    block_row = dest_block % TB_DEV
    place = jnp.where(member == 0, owners // members * TB_DEV + block_row, (member << 16) | row)
    row_total = planes * CAP
    spots = jnp.arange(members * row_total, dtype=jnp.int32)
    taken = (member * row_total + row)[None, :] == spots[:, None]
    labels = jnp.sum(jnp.where(taken, block_row[None, :] + 1, 0), axis=1) - 1
    labels = [swap(labels[q * row_total : (q + 1) * row_total], q) for q in range(1, members)]
    area = PATCH * PATCH
    weight = embed_weight.reshape(channels, area, emb).transpose(1, 0, 2)
    lists, place, weight, *labels = lax.optimization_barrier((lists, place, weight, *labels))

    own_shape = pltpu.VMEM((planes * TB_DEV, channels, block_size), jnp.float32)
    row_shape = jax.ShapeDtypeStruct((row_total, channels, block_size), jnp.bfloat16)
    own, *rows = pl.pallas_call(
        functools.partial(late_kernel, tiles, slots),
        out_shape=(own_shape,) + (row_shape,) * (members - 1),
        in_specs=[SMEM, SMEM, VMEM, VMEM, VMEM],
        out_specs=(VMEM,) * members,
        scratch_shapes=[pltpu.VMEM(acc_shape, jnp.float32)],
        compiler_params=limit(12),
        cost_estimate=pl.CostEstimate(
            flops=tiles * channels * block_size * block_size,
            bytes_accessed=2 * channels * width * 2,
            transcendentals=0,
        ),
        name="late_tiles",
    )(lists, place, far, in_vmem(partial), in_vmem(held))

    rows = [swap(r, q + 1) for q, r in enumerate(rows)]
    part = (TB_DEV, channels, block_size)
    by_swap = planes <= 4
    if by_swap:
        part_shapes = (pltpu.VMEM(part, jnp.float32),)
        part_shapes += (jax.ShapeDtypeStruct(part, jnp.bfloat16),) * (planes - 1)
    else:
        part_shapes = (jax.ShapeDtypeStruct((planes * TB_DEV,) + part[1:], jnp.bfloat16),)
    parts = pl.pallas_call(
        functools.partial(plane_kernel, planes),
        out_shape=part_shapes,
        in_specs=[SMEM] * members + [VMEM] * members,
        out_specs=(VMEM,) * len(part_shapes),
        scratch_shapes=[pltpu.VMEM(own_shape.shape, jnp.float32)],
        compiler_params=limit(24),
        name="plane_sum",
    )((me // members)[None], *labels, in_vmem(own), *rows)
    if by_swap:
        parts = [parts[0]] + [swap(p, (m + 1) * members) for m, p in enumerate(parts[1:])]
    else:
        columns = [[z * members + i for z in range(planes)] for i in range(members)]
        parts = [lax.all_to_all(parts[0], "dom", 0, 0, tiled=True, axis_index_groups=columns)]

    per_block = block_size // area
    return pl.pallas_call(
        final_kernel,
        out_shape=(
            jax.ShapeDtypeStruct(part, jnp.bfloat16),
            jax.ShapeDtypeStruct((TB_DEV * per_block, emb), jnp.bfloat16),
        ),
        in_specs=[VMEM] * (3 + len(parts)),
        out_specs=(VMEM, VMEM),
        scratch_shapes=[pltpu.VMEM((TB_DEV, block_size, channels), jnp.float32)],
        compiler_params=limit(16),
        name="embed",
    )(chooser(block_size), weight, embed_bias.reshape(1, emb), *parts)


def solution(mesh):
    placed = (
        P(None, ("groups", "dom")),
        P("dom", None, None),
        P("dom"),
        P("dom"),
        P("dom"),
        P("dom"),
        P(),
        P(),
    )
    return jax.shard_map(
        local,
        mesh=mesh,
        in_specs=placed,
        out_specs=(P(("groups", "dom"), None, None), P(("groups", "dom"), None)),
        check_vma=False,
    )
```

```python
import functools

import jax
import jax.numpy as jnp
from jax import lax
from jax.experimental import pallas as pl
from jax.experimental.pallas import tpu as pltpu
from jax.sharding import PartitionSpec as P

PATCH = 4
CAP = 2
TB_DEV = 4
LANES = 128
SEG = 4
UNROLL = 8
CHUNK = 64
VMEM = pl.BlockSpec(memory_space=pltpu.VMEM)
SMEM = pl.BlockSpec(memory_space=pltpu.SMEM)
ANY = pl.BlockSpec(memory_space=pl.ANY)


def up(n, step):
    return -(-n // step) * step


def list_rows(tiles, slots):
    entries = up(up(tiles + slots * (SEG - 1), SEG * UNROLL), LANES) // LANES
    return entries, -(-entries // SEG)


def iota(shape, dim):
    return lax.broadcasted_iota(jnp.int32, shape, dim)


def ones_of(mask):
    return jnp.where(mask, 1.0, 0.0)


def dot(a, b, dims):
    return lax.dot_general(
        a.astype(jnp.bfloat16),
        b.astype(jnp.bfloat16),
        (dims, ((), ())),
        preferred_element_type=jnp.float32,
    )


def store_row(out, row, values):
    for r in range(values.shape[1] // LANES):
        out[row + r : row + r + 1, :] = values[:, r * LANES : (r + 1) * LANES]


def schedule(block, slot, kinds, slots, outs):
    tiles = block.shape[1]
    bits = tiles.bit_length()
    entries, segments = list_rows(tiles, slots)
    slot_is = slot == iota((slots, tiles), 0)
    chosen = [slot_is & kind for kind in kinds]
    before = ones_of(iota((tiles, tiles), 0) < iota((tiles, tiles), 1))
    ranks = dot(jnp.concatenate([ones_of(c) for c in chosen], axis=0), before, ((1,), (0,)))
    upto = ones_of(iota((slots, slots), 1) <= iota((slots, slots), 0))
    count = tiles - iota((1, tiles), 1)
    for k, (mask, out) in enumerate(zip(chosen, outs)):
        rank = ranks[k * slots : (k + 1) * slots]
        total = jnp.sum(ones_of(mask), axis=1, keepdims=True).astype(jnp.int32)
        length = jnp.broadcast_to((total + (SEG - 1)) // SEG, (slots, LANES))
        ends = dot(upto, length.astype(jnp.float32), ((1,), (0,))).astype(jnp.int32)
        begins = (ends - length)[:, :1].astype(jnp.float32)
        place = jnp.sum(jnp.where(mask, rank + begins * SEG + 1.0, 0.0), axis=0, keepdims=True)
        place = place.astype(jnp.int32) - 1
        at_row = (place >> 7) == iota((up(entries, 8), tiles), 0)
        at_lane = ones_of((place & (LANES - 1)) == iota((LANES, tiles), 0))

        def listed(value):
            rows = jnp.where(at_row, value.astype(jnp.float32), 0.0)
            return dot(rows, at_lane, ((1,), (1,)))[:entries].astype(jnp.int32)

        out[:entries, :] = (listed(block) << bits) | (listed(count >> 5) << 5) | listed(count & 31)
        passed = ones_of(ends[:, :1] <= iota((slots, segments * LANES), 1))
        owner = jnp.sum(passed, axis=0, keepdims=True).astype(jnp.int32)
        store_row(out, entries, jnp.minimum(owner, slots - 1))
        out[entries + segments : entries + segments + 1, :] = ends[slots - 1 : slots, :]


def slot_places(dest, me, members):
    slots = dest.shape[1]
    a, b = iota((slots, slots), 0), iota((slots, slots), 1)
    column = jnp.sum(jnp.where(a == b, dest.astype(jnp.float32), 0.0), axis=1, keepdims=True)
    column = column.astype(jnp.int32)
    owner = column // TB_DEV
    earlier = ones_of((owner == dest // TB_DEV) & (b < a))
    rank = jnp.sum(earlier, axis=1, keepdims=True).astype(jnp.int32)
    return owner & (members - 1), (owner // members) ^ (me // members), rank, column & (TB_DEV - 1)


def inverse(spot, valid, value, default, width):
    hit = valid & (spot == iota((spot.shape[0], up(width, LANES)), 1))
    found = jnp.sum(jnp.where(hit, (value - default).astype(jnp.float32), 0.0), axis=0, keepdims=True)
    return found.astype(jnp.int32) + default


def run_segments(tiles, slots, meta, x, w, acc):
    entries, segments = list_rows(tiles, slots)
    bits = tiles.bit_length()
    total = meta[entries + segments, 0]

    def step(i, carry):
        results = []
        for u in range(UNROLL):
            first = (i * UNROLL + u) * SEG
            row, lane = first >> 7, first & (LANES - 1)
            xs, ws = [], []
            for k in range(SEG):
                code = meta[row, lane + k]
                column = pl.multiple_of((code >> bits) * LANES, LANES)
                xs.append(x[:, pl.ds(column, LANES)])
                ws.append(w[tiles - (code & ((1 << bits) - 1))])
            results.append(
                jnp.dot(
                    jnp.concatenate(xs, axis=1),
                    jnp.concatenate(ws, axis=0),
                    preferred_element_type=jnp.float32,
                )
            )
        for u in range(UNROLL):
            g = i * UNROLL + u
            slot = meta[entries + (g >> 7), g & (LANES - 1)]
            acc[slot] += results[u]
        return carry

    lax.fori_loop(0, (total + UNROLL - 1) // UNROLL, step, 0)


def early_kernel(members, spans, me, count, *refs):
    n = len(spans)
    tile_source, tile_slot, dest, source, near, weights = refs[:6]
    peer_dests, refs = refs[6 : 5 + members], refs[5 + members :]
    acc, held, late_lists, spots, refs = refs[0], refs[1], refs[2 : 2 + n], refs[2 + n : 2 + 2 * n], refs[2 + 2 * n :]
    x, ids, lists, meta_a, meta_b, sems, weight_sems = refs
    tiles, slots = tile_source.shape[1], dest.shape[1]
    cells = source.shape[1]
    live, me, core = count[0], me[0], me[0] & 1
    chunks = tiles // CHUNK

    def copy(c):
        part = pl.ds(c * CHUNK, CHUNK)
        return pltpu.make_async_copy(weights.at[part], held.at[part], weight_sems.at[c])

    ids_in = [
        pltpu.make_async_copy(tile_source, ids.at[0], sems.at[0]),
        pltpu.make_async_copy(tile_slot, ids.at[1], sems.at[1]),
    ]
    for c in ids_in:
        c.start()
    for c in range(chunks):
        pl.when(c * CHUNK < live)(lambda c=c: copy(c).start())
    half = cells // 2
    first = pl.multiple_of(core * half, LANES)
    cells_in = [
        pltpu.make_async_copy(source, x.at[:, pl.ds(0, cells)], sems.at[2]),
        pltpu.make_async_copy(near.at[:, pl.ds(first, half)], x.at[:, pl.ds(cells, half)], sems.at[3]),
    ]
    for c in cells_in:
        c.start()
    for c in ids_in:
        c.wait()

    own = cells // LANES
    rim = own // 2
    place = ids[0]
    on_left, on_right = place < rim, place >= rim + own
    inner = ~(on_left | on_right)
    at_hand = inner | (on_left & (core == 1)) | (on_right & (core == 0))
    offset = jnp.where(on_right, place - own - rim, place)
    block = jnp.where(inner, place - rim, jnp.where(at_hand, own + offset, offset))
    tile_ids = iota((1, tiles), 1)
    alive = tile_ids < live
    member, plane, rank, block_row = slot_places(dest[...], me, members)
    member = member ^ (me & (members - 1))
    kinds = [alive & at_hand & (tile_ids < tiles // 2), alive & at_hand & (tile_ids >= tiles // 2)]
    kinds += [alive & ~at_hand & (plane >= lo) & (plane < hi) for lo, hi in spans]
    schedule(block, ids[1], kinds, slots, (lists.at[0], lists.at[1], *late_lists))
    to_scalars = [
        pltpu.make_async_copy(lists.at[0], meta_a, sems.at[4]),
        pltpu.make_async_copy(lists.at[1], meta_b, sems.at[5]),
    ]
    for c in to_scalars:
        c.start()

    entries, segments = list_rows(tiles, slots)
    peer_places = [slot_places(d[...], me, members) for d in peer_dests]
    for (lo, hi), late_list, spot in zip(spans, late_lists, spots):
        dense, rows = (hi - lo) * TB_DEV, (hi - lo) * CAP
        inside = (plane >= lo) & (plane < hi)
        goes = jnp.where(
            member == 0,
            (plane - lo) * TB_DEV + block_row,
            dense + (member - 1) * rows + (plane - lo) * CAP + rank,
        )
        width = dense + (members - 1) * rows
        slot_ids = iota((slots, 1), 0)
        store_row(late_list, entries + segments + 1, inverse(goes, inside, slot_ids, slots, width))
        total = None
        for q, (peer_member, peer_plane, peer_rank, peer_row) in enumerate(peer_places):
            inside = (peer_plane >= lo) & (peer_plane < hi) & (peer_member == (me & (members - 1)))
            comes = q * rows + (peer_plane - lo) * CAP + peer_rank
            value = (peer_plane - lo) * TB_DEV + peer_row
            found = inverse(comes, inside, value - dense, 0, (members - 1) * rows)
            total = found if total is None else total + found
        store_row(spot, 0, total + dense)

    acc[...] = jnp.zeros_like(acc)
    held[tiles] = jnp.zeros(held.shape[1:], held.dtype)
    for c in (*cells_in, *to_scalars):
        c.wait()
    for part, meta in ((0, meta_a), (1, meta_b)):
        for c in range(part * chunks // 2, (part + 1) * chunks // 2):
            pl.when(c * CHUNK < live)(lambda c=c: copy(c).wait())
        run_segments(tiles, slots, meta, x, held, acc)


def late_kernel(tiles, slots, meta, far, partial, held, *rest):
    *outs, acc = rest
    acc[:slots] = partial[...]
    acc[slots] = jnp.zeros(acc.shape[1:], acc.dtype)
    run_segments(tiles, slots, meta, far, held, acc)
    spot = sum(list_rows(tiles, slots)) + 1
    p = 0
    for out in outs:
        for r in range(out.shape[0]):
            out[r] = acc[meta[spot + p // LANES, p % LANES]].astype(out.dtype)
            p += 1


def plane_kernel(members, me, spots, own, *refs):
    rows, outs, total = refs[: members - 1], refs[members - 1 : -1], refs[-1]
    dense = own.shape[0]
    total[:dense] = own[...]
    p = 0
    for row in rows:
        for r in range(row.shape[0]):
            total[spots[p // LANES, p % LANES]] += row[r].astype(jnp.float32)
            p += 1
    if len(outs) == 1:
        planes = dense // TB_DEV
        for m in range(planes):
            at = pl.ds((me[0] ^ m) * TB_DEV, TB_DEV)
            outs[0][at] = total[m * TB_DEV : (m + 1) * TB_DEV].astype(outs[0].dtype)
    else:
        for m, out in enumerate(outs):
            out[...] = total[m * TB_DEV : (m + 1) * TB_DEV].astype(out.dtype)


def final_kernel(choose, weight, bias, *refs):
    *parts, remapped, embedded, turned = refs
    blocks, channels, cells = remapped.shape
    for b in range(blocks):
        value = sum(p[i + b].astype(jnp.float32) for p in parts for i in range(0, p.shape[0], blocks))
        value = value.astype(jnp.bfloat16)
        remapped[b] = value
        turned[b] = lax.dot_general(
            choose[...], value, (((1,), (1,)), ((), ())), preferred_element_type=jnp.float32
        )
    per_block = cells // (PATCH * PATCH)
    total = jnp.broadcast_to(bias[...], (blocks * per_block, bias.shape[1]))
    for s in range(PATCH * PATCH):
        rows = turned[:, s * per_block : (s + 1) * per_block, :]
        rows = rows.reshape(blocks * per_block, channels).astype(jnp.bfloat16)
        total = total + jnp.dot(rows, weight[s], preferred_element_type=jnp.float32)
    embedded[...] = total.astype(jnp.bfloat16)


def chooser(cells):
    per_block = cells // (PATCH * PATCH)
    row = jnp.arange(cells, dtype=jnp.int32)
    r, q, p = row // (PATCH * per_block), row // per_block % PATCH, row % per_block
    wanted = r * (PATCH * per_block) + p * PATCH + q
    return (wanted[:, None] == jnp.arange(cells, dtype=jnp.int32)[None, :]).astype(jnp.bfloat16)


def in_vmem(x):
    return pltpu.with_memory_space_constraint(x, pltpu.VMEM)


def in_hbm(x):
    return pltpu.with_memory_space_constraint(x, pltpu.HBM)


def limit(mib):
    return pltpu.CompilerParams(vmem_limit_bytes=mib << 20)


def local(
    source, tile_weight, tile_source, tile_slot, tile_count, dest_block, embed_weight, embed_bias
):
    channels, own_cells = source.shape
    tiles, block_size, _ = tile_weight.shape
    slots = dest_block.shape[0]
    peers = lax.axis_size("dom")
    me = lax.axis_index("dom").astype(jnp.int32)
    core = me & 1
    width = own_cells // 2
    emb = embed_weight.shape[1]
    members = 4 if peers == 16 else 2
    planes = peers // members

    def swap(x, q):
        return lax.ppermute(x, "dom", [(i, i ^ q) for i in range(peers)])

    near = swap(source, 1)
    far = lax.ppermute(
        lax.dynamic_slice_in_dim(source, core * width, width, axis=1),
        "dom",
        [(i, (i + (1 if i % 2 else -1)) % peers) for i in range(peers)],
    )

    peer_dests = [swap(dest_block, q)[None, :] for q in range(1, members)]

    by_swap = planes == 4
    spans = ((2, 4), (0, 2)) if by_swap else ((0, planes),)
    entries, segments = list_rows(tiles, slots)

    def table(rows):
        return jax.ShapeDtypeStruct((up(rows, 8), LANES), jnp.int32)

    def map_rows(lo, hi):
        return up((hi - lo) * (TB_DEV + (members - 1) * CAP), LANES) // LANES

    acc_shape = (slots, channels, block_size)
    list_table = table(entries + segments + 1)
    flops = tiles * channels * block_size * block_size
    partial, held, *tables = pl.pallas_call(
        functools.partial(early_kernel, members, spans),
        out_shape=(
            pltpu.VMEM(acc_shape, jnp.float32),
            pltpu.VMEM((tiles + 1, block_size, block_size), jnp.bfloat16),
            *[table(entries + segments + 1 + map_rows(*span)) for span in spans],
            *[table(map_rows(*span)) for span in spans],
        ),
        in_specs=[SMEM, SMEM, ANY, ANY, VMEM, ANY, ANY, ANY] + [VMEM] * (members - 1),
        out_specs=(VMEM,) * (2 + 2 * len(spans)),
        scratch_shapes=[
            pltpu.VMEM((channels, own_cells + width), jnp.bfloat16),
            pltpu.VMEM((2, 1, tiles), jnp.int32),
            pltpu.VMEM((2, *list_table.shape), jnp.int32),
            pltpu.SMEM(list_table.shape, jnp.int32),
            pltpu.SMEM(list_table.shape, jnp.int32),
            pltpu.SemaphoreType.DMA((6,)),
            pltpu.SemaphoreType.DMA((tiles // CHUNK,)),
        ],
        compiler_params=limit(16),
        cost_estimate=pl.CostEstimate(
            flops=2 * flops, bytes_accessed=tile_weight.size * 2, transcendentals=0
        ),
        name="early_tiles",
    )(
        me[None],
        tile_count,
        in_hbm(tile_source[None, :]),
        in_hbm(tile_slot[None, :]),
        dest_block[None, :],
        in_hbm(source),
        near,
        in_hbm(tile_weight),
        *peer_dests,
    )
    late_lists, spots = tables[: len(spans)], tables[len(spans) :]

    area = PATCH * PATCH
    partial, embed_weight = lax.optimization_barrier((partial, embed_weight))
    weight = embed_weight.reshape(channels, area, emb).transpose(1, 0, 2)
    far, weight = lax.optimization_barrier((far, weight))

    cells = (channels, block_size)
    part = (TB_DEV, *cells)
    own_rows = []
    for (lo, hi), late_list in zip(spans, late_lists):
        own_shape = pltpu.VMEM(((hi - lo) * TB_DEV, *cells), jnp.float32)
        row_shape = jax.ShapeDtypeStruct(((hi - lo) * CAP, *cells), jnp.bfloat16)
        own, *rows = pl.pallas_call(
            functools.partial(late_kernel, tiles, slots),
            out_shape=(own_shape,) + (row_shape,) * (members - 1),
            in_specs=[SMEM, VMEM, VMEM, VMEM],
            out_specs=(VMEM,) * members,
            scratch_shapes=[pltpu.VMEM((slots + 1, *cells), jnp.float32)],
            compiler_params=limit(16),
            cost_estimate=pl.CostEstimate(
                flops=flops, bytes_accessed=2 * channels * width, transcendentals=0
            ),
            name="late_tiles",
        )(late_list, far, in_vmem(partial), in_vmem(held))
        own_rows.append((own, [swap(r, q + 1) for q, r in enumerate(rows)]))

    parts = []
    for (lo, hi), spot, (own, rows) in zip(spans, spots, own_rows):
        if by_swap:
            part_shapes = [
                jax.ShapeDtypeStruct(part, jnp.bfloat16) if m else pltpu.VMEM(part, jnp.float32)
                for m in range(lo, hi)
            ]
        else:
            part_shapes = [jax.ShapeDtypeStruct(own.shape, jnp.bfloat16)]
        sums = pl.pallas_call(
            functools.partial(plane_kernel, members),
            out_shape=tuple(part_shapes),
            in_specs=[SMEM] * 2 + [VMEM] * members,
            out_specs=(VMEM,) * len(part_shapes),
            scratch_shapes=[pltpu.VMEM((own.shape[0] + 1, *cells), jnp.float32)],
            compiler_params=limit(24),
            name="plane_sum",
        )((me // members)[None], spot, in_vmem(own), *rows)
        if by_swap:
            parts += [swap(s, m * members) if m else s for m, s in zip(range(lo, hi), sums)]
        else:
            columns = [[z * members + i for z in range(planes)] for i in range(members)]
            parts.append(lax.all_to_all(sums[0], "dom", 0, 0, tiled=True, axis_index_groups=columns))

    per_block = block_size // area
    return pl.pallas_call(
        final_kernel,
        out_shape=(
            jax.ShapeDtypeStruct(part, jnp.bfloat16),
            jax.ShapeDtypeStruct((TB_DEV * per_block, emb), jnp.bfloat16),
        ),
        in_specs=[VMEM] * (3 + len(parts)),
        out_specs=(VMEM, VMEM),
        scratch_shapes=[pltpu.VMEM((TB_DEV, block_size, channels), jnp.float32)],
        compiler_params=limit(16),
        name="embed",
    )(chooser(block_size), weight, embed_bias.reshape(1, emb), *parts)


def solution(mesh):
    placed = (
        P(None, ("groups", "dom")),
        P("dom", None, None),
        P("dom"),
        P("dom"),
        P("dom"),
        P("dom"),
        P(),
        P(),
    )
    return jax.shard_map(
        local,
        mesh=mesh,
        in_specs=placed,
        out_specs=(P(("groups", "dom"), None, None), P(("groups", "dom"), None)),
        check_vma=False,
    )
```

```python
import functools

import jax
import jax.numpy as jnp
from jax import lax
from jax.experimental import pallas as pl
from jax.experimental.pallas import tpu as pltpu
from jax.sharding import PartitionSpec as P

PATCH = 4
CAP = 2
TB_DEV = 4
LANES = 128
SEG = 4
UNROLL = 8
CHUNK = 64
VMEM = pl.BlockSpec(memory_space=pltpu.VMEM)
SMEM = pl.BlockSpec(memory_space=pltpu.SMEM)
ANY = pl.BlockSpec(memory_space=pl.ANY)


def up(n, step):
    return -(-n // step) * step


def list_rows(tiles, slots):
    entries = up(up(tiles + slots * (SEG - 1), SEG * UNROLL), LANES) // LANES
    return entries, -(-entries // SEG)


def iota(shape, dim):
    return lax.broadcasted_iota(jnp.int32, shape, dim)


def ones_of(mask):
    return jnp.where(mask, 1.0, 0.0)


def dot(a, b, dims):
    return lax.dot_general(
        a.astype(jnp.bfloat16),
        b.astype(jnp.bfloat16),
        (dims, ((), ())),
        preferred_element_type=jnp.float32,
    )


def store_row(out, row, values):
    for r in range(values.shape[1] // LANES):
        out[row + r : row + r + 1, :] = values[:, r * LANES : (r + 1) * LANES]


def schedule(block, slot, kinds, slots, outs):
    tiles = block.shape[1]
    bits = tiles.bit_length()
    entries, segments = list_rows(tiles, slots)
    bins = len(kinds) * slots
    slot_is = slot == iota((slots, tiles), 0)
    chosen = jnp.concatenate([ones_of(slot_is & kind) for kind in kinds], axis=0)
    before = ones_of(iota((tiles, tiles), 0) < iota((tiles, tiles), 1))
    rank = dot(chosen, before, ((1,), (0,)))
    total = jnp.sum(chosen, axis=1, keepdims=True).astype(jnp.int32)
    length = jnp.broadcast_to((total + (SEG - 1)) // SEG, (bins, LANES))
    a, b = iota((bins, bins), 0), iota((bins, bins), 1)
    upto = ones_of((b <= a) & (b // slots == a // slots))
    ends = dot(upto, length.astype(jnp.float32), ((1,), (0,))).astype(jnp.int32)
    begins = (ends - length)[:, :1] * SEG + iota((bins, 1), 0) // slots * (entries * LANES)
    place = jnp.sum(chosen * (rank + begins.astype(jnp.float32) + 1.0), axis=0, keepdims=True)
    place = place.astype(jnp.int32) - 1
    rows = up(len(kinds) * entries, 8)
    at_row = ones_of((place >> 7) == iota((rows, tiles), 0))
    at_lane = ones_of((place & (LANES - 1)) == iota((LANES, tiles), 0))
    count = tiles - iota((1, tiles), 1)
    values = [at_row * v.astype(jnp.float32) for v in (block, count >> 5, count & 31)]
    found = dot(jnp.concatenate(values, axis=0), at_lane, ((1,), (1,))).astype(jnp.int32)
    code = (found[:rows] << bits) | (found[rows : 2 * rows] << 5) | found[2 * rows :]
    for k, out in enumerate(outs):
        mine = ends[k * slots : (k + 1) * slots]
        out[:entries, :] = code[k * entries : (k + 1) * entries]
        passed = ones_of(mine[:, :1] <= iota((slots, segments * LANES), 1))
        owner = jnp.sum(passed, axis=0, keepdims=True).astype(jnp.int32)
        store_row(out, entries, jnp.minimum(owner, slots - 1))
        out[entries + segments : entries + segments + 1, :] = mine[slots - 1 :]


def slot_places(dest, me, members):
    slots = dest.shape[1]
    a, b = iota((slots, slots), 0), iota((slots, slots), 1)
    column = jnp.sum(jnp.where(a == b, dest.astype(jnp.float32), 0.0), axis=1, keepdims=True)
    column = column.astype(jnp.int32)
    owner = column // TB_DEV
    earlier = ones_of((owner == dest // TB_DEV) & (b < a))
    rank = jnp.sum(earlier, axis=1, keepdims=True).astype(jnp.int32)
    return owner & (members - 1), (owner // members) ^ (me // members), rank, column & (TB_DEV - 1)


def run_segments(tiles, slots, meta, x, w, acc):
    entries, segments = list_rows(tiles, slots)
    bits = tiles.bit_length()
    total = meta[entries + segments, 0]

    def step(i, carry):
        results = []
        for u in range(UNROLL):
            first = (i * UNROLL + u) * SEG
            row, lane = first >> 7, first & (LANES - 1)
            xs, ws = [], []
            for k in range(SEG):
                code = meta[row, lane + k]
                column = pl.multiple_of((code >> bits) * LANES, LANES)
                xs.append(x[:, pl.ds(column, LANES)])
                ws.append(w[tiles - (code & ((1 << bits) - 1))])
            results.append(
                jnp.dot(
                    jnp.concatenate(xs, axis=1),
                    jnp.concatenate(ws, axis=0),
                    preferred_element_type=jnp.float32,
                )
            )
        for u in range(UNROLL):
            g = i * UNROLL + u
            slot = meta[entries + (g >> 7), g & (LANES - 1)]
            acc[slot] += results[u]
        return carry

    lax.fori_loop(0, (total + UNROLL - 1) // UNROLL, step, 0)


def early_kernel(members, spans, me, count, *refs):
    tile_source, tile_slot, dest, source, near, weights, acc, held, late_list, *refs = refs
    labels, (x, ids, dests, lists, meta_a, meta_b, sems, weight_sems) = refs[: len(spans)], refs[len(spans) :]
    tiles, slots = tile_source.shape[1], dest.shape[1]
    cells = source.shape[1]
    live, me, core = count[0], me[0], me[0] & 1
    chunks = tiles // CHUNK

    def copy(c):
        part = pl.ds(c * CHUNK, CHUNK)
        return pltpu.make_async_copy(weights.at[part], held.at[part], weight_sems.at[c])

    ids_in = [
        pltpu.make_async_copy(tile_source, ids.at[0], sems.at[0]),
        pltpu.make_async_copy(tile_slot, ids.at[1], sems.at[1]),
        pltpu.make_async_copy(dest, dests, sems.at[6]),
    ]
    for c in ids_in:
        c.start()
    for c in range(chunks):
        pl.when(c * CHUNK < live)(lambda c=c: copy(c).start())
    half = cells // 2
    first = pl.multiple_of(core * half, LANES)
    cells_in = [
        pltpu.make_async_copy(source, x.at[:, pl.ds(0, cells)], sems.at[2]),
        pltpu.make_async_copy(near.at[:, pl.ds(first, half)], x.at[:, pl.ds(cells, half)], sems.at[3]),
    ]
    for c in cells_in:
        c.start()
    for c in ids_in:
        c.wait()

    own = cells // LANES
    rim = own // 2
    place = ids[0]
    on_left, on_right = place < rim, place >= rim + own
    inner = ~(on_left | on_right)
    at_hand = inner | (on_left & (core == 1)) | (on_right & (core == 0))
    offset = jnp.where(on_right, place - own - rim, place)
    block = jnp.where(inner, place - rim, jnp.where(at_hand, own + offset, offset))
    tile_ids = iota((1, tiles), 1)
    alive = tile_ids < live
    member, plane, rank, block_row = slot_places(dests[...], me, members)
    member = member ^ (me & (members - 1))
    kinds = [alive & at_hand & (tile_ids < tiles // 2), alive & at_hand & (tile_ids >= tiles // 2)]
    kinds += [alive & ~at_hand]
    schedule(block, ids[1], kinds, slots, (lists.at[0], lists.at[1], late_list))
    to_scalars = [
        pltpu.make_async_copy(lists.at[0], meta_a, sems.at[4]),
        pltpu.make_async_copy(lists.at[1], meta_b, sems.at[5]),
    ]
    for c in to_scalars:
        c.start()

    entries, segments = list_rows(tiles, slots)
    first, goes = 0, jnp.zeros((slots, 1), jnp.int32)
    for (lo, hi), label in zip(spans, labels):
        dense, rows = (hi - lo) * TB_DEV, (hi - lo) * CAP
        inside = (plane >= lo) & (plane < hi)
        spot = (plane - lo) * CAP + rank
        place = jnp.where(member == 0, (plane - lo) * TB_DEV + block_row, dense + (member - 1) * rows + spot)
        goes = jnp.where(inside, first + place, goes)
        first += dense + (members - 1) * rows
        for q in range(1, members):
            hit = inside & (member == q) & (spot == iota((slots, label.shape[1]), 1))
            found = dot(ones_of(hit), jnp.broadcast_to(block_row + 1, (slots, LANES)), ((0,), (0,)))
            label[q - 1] = (found - 1.0).astype(label.dtype)
    hit = goes == iota((slots, up(first, LANES)), 1)
    sources = jnp.sum(jnp.where(hit, (iota((slots, 1), 0) - slots).astype(jnp.float32), 0.0), axis=0, keepdims=True)
    store_row(late_list, entries + segments + 1, sources.astype(jnp.int32) + slots)

    acc[...] = jnp.zeros_like(acc)
    held[tiles] = jnp.zeros(held.shape[1:], held.dtype)
    for c in (*cells_in, *to_scalars):
        c.wait()
    for part, meta in ((0, meta_a), (1, meta_b)):
        for c in range(part * chunks // 2, (part + 1) * chunks // 2):
            pl.when(c * CHUNK < live)(lambda c=c: copy(c).wait())
        run_segments(tiles, slots, meta, x, held, acc)


def late_kernel(tiles, slots, members, meta, far, partial, held, *rest):
    n = (len(rest) - 1) // (members + 1)
    labels, outs, acc = rest[:n], rest[n:-1], rest[-1]
    acc[:slots] = partial[...]
    acc[slots] = jnp.zeros(acc.shape[1:], acc.dtype)
    run_segments(tiles, slots, meta, far, held, acc)
    spot = sum(list_rows(tiles, slots)) + 1
    p = 0

    def next_slot():
        nonlocal p
        p += 1
        return acc[meta[spot + (p - 1) // LANES, (p - 1) % LANES]]

    for i, label in enumerate(labels):
        own, *rows = outs[i * members : (i + 1) * members]
        dense, pair = own.shape[0], CAP * own.shape[1]
        planes = dense // TB_DEV
        for r in range(dense):
            own[r] = next_slot()
        for q, out in enumerate(rows):
            for m in range(planes):
                both = jnp.concatenate([next_slot() for _ in range(CAP)], axis=0)
                out[m * pair : (m + 1) * pair, :] = both.astype(out.dtype)
            out[planes * pair :, :] = label[q]


def plane_kernel(members, me, own, *refs):
    rows, outs = refs[: members - 1], refs[members - 1 :]
    dense, channels, cells = own.shape
    planes, pair = dense // TB_DEV, CAP * channels
    labels = [row[planes * pair :, :].astype(jnp.float32) for row in rows]
    for m in range(planes):
        sums = [own[m * TB_DEV + k] for k in range(TB_DEV)]
        for row, label in zip(rows, labels):
            both = row[m * pair : (m + 1) * pair, :].astype(jnp.float32)
            for c in range(CAP):
                value = both[c * channels : (c + 1) * channels]
                mark = jnp.broadcast_to(label[m * CAP + c : m * CAP + c + 1], (channels, cells))
                sums = [s + jnp.where(mark == k, value, 0.0) for k, s in enumerate(sums)]
        for k, s in enumerate(sums):
            if len(outs) == 1:
                outs[0][(me[0] ^ m) * TB_DEV + k] = s.astype(outs[0].dtype)
            else:
                outs[m][k] = s.astype(outs[m].dtype)


def final_kernel(choose, weight, bias, *refs):
    *parts, remapped, embedded, turned = refs
    blocks, channels, cells = remapped.shape
    for b in range(blocks):
        value = sum(p[i + b].astype(jnp.float32) for p in parts for i in range(0, p.shape[0], blocks))
        value = value.astype(jnp.bfloat16)
        remapped[b] = value
        turned[b] = lax.dot_general(
            choose[...], value, (((1,), (1,)), ((), ())), preferred_element_type=jnp.float32
        )
    per_block = cells // (PATCH * PATCH)
    total = jnp.broadcast_to(bias[...], (blocks * per_block, bias.shape[1]))
    for s in range(PATCH * PATCH):
        rows = turned[:, s * per_block : (s + 1) * per_block, :]
        rows = rows.reshape(blocks * per_block, channels).astype(jnp.bfloat16)
        total = total + jnp.dot(rows, weight[s], preferred_element_type=jnp.float32)
    embedded[...] = total.astype(jnp.bfloat16)


def chooser(cells):
    per_block = cells // (PATCH * PATCH)
    row = jnp.arange(cells, dtype=jnp.int32)
    r, q, p = row // (PATCH * per_block), row // per_block % PATCH, row % per_block
    wanted = r * (PATCH * per_block) + p * PATCH + q
    return (wanted[:, None] == jnp.arange(cells, dtype=jnp.int32)[None, :]).astype(jnp.bfloat16)


def in_vmem(x):
    return pltpu.with_memory_space_constraint(x, pltpu.VMEM)


def in_hbm(x):
    return pltpu.with_memory_space_constraint(x, pltpu.HBM)


def limit(mib):
    return pltpu.CompilerParams(vmem_limit_bytes=mib << 20)


def local(
    source, tile_weight, tile_source, tile_slot, tile_count, dest_block, embed_weight, embed_bias
):
    channels, own_cells = source.shape
    tiles, block_size, _ = tile_weight.shape
    slots = dest_block.shape[0]
    peers = lax.axis_size("dom")
    me = lax.axis_index("dom").astype(jnp.int32)
    core = me & 1
    width = own_cells // 2
    emb = embed_weight.shape[1]
    members = 4 if peers == 16 else 2
    planes = peers // members

    def swap(x, q):
        return lax.ppermute(x, "dom", [(i, i ^ q) for i in range(peers)])

    near = swap(source, 1)
    far = lax.ppermute(
        lax.dynamic_slice_in_dim(source, core * width, width, axis=1),
        "dom",
        [(i, (i + (1 if i % 2 else -1)) % peers) for i in range(peers)],
    )

    by_swap = planes == 4
    spans = ((0, 2), (2, 4)) if by_swap else ((0, planes),)
    entries, segments = list_rows(tiles, slots)

    def table(rows):
        return jax.ShapeDtypeStruct((up(rows, 8), LANES), jnp.int32)

    def label_shape(lo, hi):
        return (members - 1, up((hi - lo) * CAP, 16), LANES)

    acc_shape = (slots, channels, block_size)
    list_table = table(entries + segments + 1)
    map_rows = up(planes * (TB_DEV + (members - 1) * CAP), LANES) // LANES
    flops = tiles * channels * block_size * block_size
    partial, held, late_list, *labels = pl.pallas_call(
        functools.partial(early_kernel, members, spans),
        out_shape=(
            pltpu.VMEM(acc_shape, jnp.float32),
            pltpu.VMEM((tiles + 1, block_size, block_size), jnp.bfloat16),
            table(entries + segments + 1 + map_rows),
            *[jax.ShapeDtypeStruct(label_shape(*span), jnp.bfloat16) for span in spans],
        ),
        in_specs=[SMEM, SMEM] + [ANY] * 6,
        out_specs=(VMEM,) * (3 + len(spans)),
        scratch_shapes=[
            pltpu.VMEM((channels, own_cells + width), jnp.bfloat16),
            pltpu.VMEM((2, 1, tiles), jnp.int32),
            pltpu.VMEM((1, slots), jnp.int32),
            pltpu.VMEM((2, *list_table.shape), jnp.int32),
            pltpu.SMEM(list_table.shape, jnp.int32),
            pltpu.SMEM(list_table.shape, jnp.int32),
            pltpu.SemaphoreType.DMA((7,)),
            pltpu.SemaphoreType.DMA((tiles // CHUNK,)),
        ],
        compiler_params=limit(8),
        cost_estimate=pl.CostEstimate(
            flops=2 * flops, bytes_accessed=tile_weight.size * 2, transcendentals=0
        ),
        name="early_tiles",
    )(
        me[None],
        tile_count,
        in_hbm(tile_source[None, :]),
        in_hbm(tile_slot[None, :]),
        in_hbm(dest_block[None, :]),
        in_hbm(source),
        near,
        in_hbm(tile_weight),
    )

    area = PATCH * PATCH
    partial, embed_weight = lax.optimization_barrier((partial, embed_weight))
    weight = embed_weight.reshape(channels, area, emb).transpose(1, 0, 2)
    far, weight = lax.optimization_barrier((far, weight))

    cells = (channels, block_size)
    part = (TB_DEV, *cells)
    late_shapes = []
    for (lo, hi), label in zip(spans, labels):
        row_total = (hi - lo) * CAP * channels + label.shape[1]
        late_shapes.append(pltpu.VMEM(((hi - lo) * TB_DEV, *cells), jnp.float32))
        late_shapes += [jax.ShapeDtypeStruct((row_total, block_size), jnp.bfloat16)] * (members - 1)
    late = pl.pallas_call(
        functools.partial(late_kernel, tiles, slots, members),
        out_shape=tuple(late_shapes),
        in_specs=[SMEM] + [VMEM] * (3 + len(labels)),
        out_specs=(VMEM,) * len(late_shapes),
        scratch_shapes=[pltpu.VMEM((slots + 1, *cells), jnp.float32)],
        compiler_params=limit(6),
        cost_estimate=pl.CostEstimate(
            flops=flops, bytes_accessed=2 * channels * width, transcendentals=0
        ),
        name="late_tiles",
    )(late_list, far, in_vmem(partial), in_vmem(held), *labels)
    own_rows = []
    for i in range(len(spans)):
        own, *rows = late[i * members : (i + 1) * members]
        own_rows.append((own, [swap(r, q + 1) for q, r in enumerate(rows)]))

    parts = []
    for (lo, hi), (own, rows) in zip(spans, own_rows):
        if by_swap:
            part_shapes = [
                jax.ShapeDtypeStruct(part, jnp.bfloat16) if m else pltpu.VMEM(part, jnp.float32)
                for m in range(lo, hi)
            ]
        else:
            part_shapes = [jax.ShapeDtypeStruct(own.shape, jnp.bfloat16)]
        sums = pl.pallas_call(
            functools.partial(plane_kernel, members),
            out_shape=tuple(part_shapes),
            in_specs=[SMEM] + [VMEM] * members,
            out_specs=(VMEM,) * len(part_shapes),
            compiler_params=limit(4),
            name="plane_sum",
        )((me // members)[None], in_vmem(own), *rows)
        if by_swap:
            parts += [swap(s, m * members) if m else s for m, s in zip(range(lo, hi), sums)]
        else:
            columns = [[z * members + i for z in range(planes)] for i in range(members)]
            parts.append(lax.all_to_all(sums[0], "dom", 0, 0, tiled=True, axis_index_groups=columns))

    per_block = block_size // area
    return pl.pallas_call(
        final_kernel,
        out_shape=(
            jax.ShapeDtypeStruct(part, jnp.bfloat16),
            jax.ShapeDtypeStruct((TB_DEV * per_block, emb), jnp.bfloat16),
        ),
        in_specs=[VMEM] * (3 + len(parts)),
        out_specs=(VMEM, VMEM),
        scratch_shapes=[pltpu.VMEM((TB_DEV, block_size, channels), jnp.float32)],
        compiler_params=limit(6),
        name="embed",
    )(chooser(block_size), weight, embed_bias.reshape(1, emb), *parts)


def solution(mesh):
    placed = (
        P(None, ("groups", "dom")),
        P("dom", None, None),
        P("dom"),
        P("dom"),
        P("dom"),
        P("dom"),
        P(),
        P(),
    )
    return jax.shard_map(
        local,
        mesh=mesh,
        in_specs=placed,
        out_specs=(P(("groups", "dom"), None, None), P(("groups", "dom"), None)),
        check_vma=False,
    )
```

```python
import functools

import jax
import jax.numpy as jnp
from jax import lax
from jax.experimental import pallas as pl
from jax.experimental.pallas import tpu as pltpu
from jax.sharding import PartitionSpec as P

PATCH = 4
CAP = 2
TB_DEV = 4
LANES = 128
SEG = 4
UNROLL = 20
CHUNK = 64
VMEM = pl.BlockSpec(memory_space=pltpu.VMEM)
SMEM = pl.BlockSpec(memory_space=pltpu.SMEM)
ANY = pl.BlockSpec(memory_space=pl.ANY)


def up(n, step):
    return -(-n // step) * step


def list_rows(tiles, slots):
    entries = up(up(tiles + slots * (SEG - 1), SEG * UNROLL), LANES) // LANES
    return entries, -(-entries // SEG)


def iota(shape, dim):
    return lax.broadcasted_iota(jnp.int32, shape, dim)


def ones_of(mask):
    return jnp.where(mask, 1.0, 0.0)


def dot(a, b, dims):
    return lax.dot_general(
        a.astype(jnp.bfloat16),
        b.astype(jnp.bfloat16),
        (dims, ((), ())),
        preferred_element_type=jnp.float32,
    )


def store_row(out, row, values):
    for r in range(values.shape[1] // LANES):
        out[row + r : row + r + 1, :] = values[:, r * LANES : (r + 1) * LANES]


def schedule(block, slot, kinds, slots, outs):
    tiles = block.shape[1]
    bits = tiles.bit_length()
    entries, segments = list_rows(tiles, slots)
    bins = len(kinds) * slots
    slot_is = slot == iota((slots, tiles), 0)
    chosen = jnp.concatenate([ones_of(slot_is & kind) for kind in kinds], axis=0)
    before = ones_of(iota((tiles, tiles), 0) < iota((tiles, tiles), 1))
    rank = dot(chosen, before, ((1,), (0,)))
    total = jnp.sum(chosen, axis=1, keepdims=True).astype(jnp.int32)
    length = jnp.broadcast_to((total + (SEG - 1)) // SEG, (bins, LANES))
    a, b = iota((bins, bins), 0), iota((bins, bins), 1)
    upto = ones_of((b <= a) & (b // slots == a // slots))
    ends = dot(upto, length.astype(jnp.float32), ((1,), (0,))).astype(jnp.int32)
    begins = (ends - length)[:, :1] * SEG + iota((bins, 1), 0) // slots * (entries * LANES)
    place = jnp.sum(chosen * (rank + begins.astype(jnp.float32) + 1.0), axis=0, keepdims=True)
    place = place.astype(jnp.int32) - 1
    rows = up(len(kinds) * entries, 8)
    at_row = ones_of((place >> 7) == iota((rows, tiles), 0))
    at_lane = ones_of((place & (LANES - 1)) == iota((LANES, tiles), 0))
    count = tiles - iota((1, tiles), 1)
    values = [at_row * v.astype(jnp.float32) for v in (block, count >> 5, count & 31)]
    found = dot(jnp.concatenate(values, axis=0), at_lane, ((1,), (1,))).astype(jnp.int32)
    code = (found[:rows] << bits) | (found[rows : 2 * rows] << 5) | found[2 * rows :]
    for k, out in enumerate(outs):
        mine = ends[k * slots : (k + 1) * slots]
        out[:entries, :] = code[k * entries : (k + 1) * entries]
        passed = ones_of(mine[:, :1] <= iota((slots, segments * LANES), 1))
        owner = jnp.sum(passed, axis=0, keepdims=True).astype(jnp.int32)
        store_row(out, entries, jnp.minimum(owner, slots - 1))
        out[entries + segments : entries + segments + 1, :] = mine[slots - 1 :]


def slot_places(dest, me, members):
    slots = dest.shape[1]
    a, b = iota((slots, slots), 0), iota((slots, slots), 1)
    column = jnp.sum(jnp.where(a == b, dest.astype(jnp.float32), 0.0), axis=1, keepdims=True)
    column = column.astype(jnp.int32)
    owner = column // TB_DEV
    earlier = ones_of((owner == dest // TB_DEV) & (b < a))
    rank = jnp.sum(earlier, axis=1, keepdims=True).astype(jnp.int32)
    return owner & (members - 1), (owner // members) ^ (me // members), rank, column & (TB_DEV - 1)


def run_segments(tiles, slots, meta, x, w, acc):
    entries, segments = list_rows(tiles, slots)
    bits = tiles.bit_length()
    total = meta[entries + segments, 0]

    def step(i, carry):
        results = []
        for u in range(UNROLL):
            first = (i * UNROLL + u) * SEG
            row, lane = first >> 7, first & (LANES - 1)
            xs, ws = [], []
            for k in range(SEG):
                code = meta[row, lane + k]
                column = pl.multiple_of((code >> bits) * LANES, LANES)
                xs.append(x[:, pl.ds(column, LANES)])
                ws.append(w[tiles - (code & ((1 << bits) - 1))])
            results.append(
                jnp.dot(
                    jnp.concatenate(xs, axis=1),
                    jnp.concatenate(ws, axis=0),
                    preferred_element_type=jnp.float32,
                )
            )
        for u in range(UNROLL):
            g = i * UNROLL + u
            slot = meta[entries + (g >> 7), g & (LANES - 1)]
            acc[slot] += results[u]
        return carry

    lax.fori_loop(0, (total + UNROLL - 1) // UNROLL, step, 0)


def early_kernel(members, spans, me, count, *refs):
    tile_source, tile_slot, dest, source, near, weights, acc, held, late_list, *refs = refs
    labels, (x, ids, dests, lists, meta_a, meta_b, sems, weight_sems) = refs[: len(spans)], refs[len(spans) :]
    tiles, slots = tile_source.shape[1], dest.shape[1]
    cells = source.shape[1]
    live, me, core = count[0], me[0], me[0] & 1
    chunks = tiles // CHUNK

    def copy(c):
        part = pl.ds(c * CHUNK, CHUNK)
        return pltpu.make_async_copy(weights.at[part], held.at[part], weight_sems.at[c])

    ids_in = [
        pltpu.make_async_copy(tile_source, ids.at[0], sems.at[0]),
        pltpu.make_async_copy(tile_slot, ids.at[1], sems.at[1]),
        pltpu.make_async_copy(dest, dests, sems.at[6]),
    ]
    for c in ids_in:
        c.start()
    for c in range(chunks):
        pl.when(c * CHUNK < live)(lambda c=c: copy(c).start())
    half = cells // 2
    first = pl.multiple_of(core * half, LANES)
    cells_in = [
        pltpu.make_async_copy(source, x.at[:, pl.ds(0, cells)], sems.at[2]),
        pltpu.make_async_copy(near.at[:, pl.ds(first, half)], x.at[:, pl.ds(cells, half)], sems.at[3]),
    ]
    for c in cells_in:
        c.start()
    for c in ids_in:
        c.wait()

    own = cells // LANES
    rim = own // 2
    place = ids[0]
    on_left, on_right = place < rim, place >= rim + own
    inner = ~(on_left | on_right)
    at_hand = inner | (on_left & (core == 1)) | (on_right & (core == 0))
    offset = jnp.where(on_right, place - own - rim, place)
    block = jnp.where(inner, place - rim, jnp.where(at_hand, own + offset, offset))
    tile_ids = iota((1, tiles), 1)
    alive = tile_ids < live
    member, plane, rank, block_row = slot_places(dests[...], me, members)
    member = member ^ (me & (members - 1))
    kinds = [alive & at_hand & (tile_ids < tiles // 2), alive & at_hand & (tile_ids >= tiles // 2)]
    kinds += [alive & ~at_hand]
    schedule(block, ids[1], kinds, slots, (lists.at[0], lists.at[1], late_list))
    to_scalars = [
        pltpu.make_async_copy(lists.at[0], meta_a, sems.at[4]),
        pltpu.make_async_copy(lists.at[1], meta_b, sems.at[5]),
    ]
    for c in to_scalars:
        c.start()

    entries, segments = list_rows(tiles, slots)
    first, goes = 0, jnp.zeros((slots, 1), jnp.int32)
    for (lo, hi), label in zip(spans, labels):
        dense, rows = (hi - lo) * TB_DEV, (hi - lo) * CAP
        inside = (plane >= lo) & (plane < hi)
        spot = (plane - lo) * CAP + rank
        place = jnp.where(member == 0, (plane - lo) * TB_DEV + block_row, dense + (member - 1) * rows + spot)
        goes = jnp.where(inside, first + place, goes)
        first += dense + (members - 1) * rows
        for q in range(1, members):
            hit = inside & (member == q) & (spot == iota((slots, label.shape[1]), 1))
            found = dot(ones_of(hit), jnp.broadcast_to(block_row + 1, (slots, LANES)), ((0,), (0,)))
            label[q - 1] = (found - 1.0).astype(label.dtype)
    hit = goes == iota((slots, up(first, LANES)), 1)
    sources = jnp.sum(jnp.where(hit, (iota((slots, 1), 0) - slots).astype(jnp.float32), 0.0), axis=0, keepdims=True)
    store_row(late_list, entries + segments + 1, sources.astype(jnp.int32) + slots)

    acc[...] = jnp.zeros_like(acc)
    held[tiles] = jnp.zeros(held.shape[1:], held.dtype)
    for c in (*cells_in, *to_scalars):
        c.wait()
    for part, meta in ((0, meta_a), (1, meta_b)):
        for c in range(part * chunks // 2, (part + 1) * chunks // 2):
            pl.when(c * CHUNK < live)(lambda c=c: copy(c).wait())
        run_segments(tiles, slots, meta, x, held, acc)


def late_kernel(tiles, slots, members, meta, far, partial, held, *rest):
    n = (len(rest) - 1) // (members + 1)
    labels, outs, acc = rest[:n], rest[n:-1], rest[-1]
    acc[:slots] = partial[...]
    acc[slots] = jnp.zeros(acc.shape[1:], acc.dtype)
    run_segments(tiles, slots, meta, far, held, acc)
    spot = sum(list_rows(tiles, slots)) + 1
    p = 0

    def next_slot():
        nonlocal p
        p += 1
        return acc[meta[spot + (p - 1) // LANES, (p - 1) % LANES]]

    for i, label in enumerate(labels):
        own, *rows = outs[i * members : (i + 1) * members]
        dense, pair = own.shape[0], CAP * own.shape[1]
        planes = dense // TB_DEV
        for r in range(dense):
            own[r] = next_slot()
        for q, out in enumerate(rows):
            for m in range(planes):
                both = jnp.concatenate([next_slot() for _ in range(CAP)], axis=0)
                out[m * pair : (m + 1) * pair, :] = both.astype(out.dtype)
            out[planes * pair :, :] = label[q]


def plane_kernel(members, me, own, *refs):
    rows, outs = refs[: members - 1], refs[members - 1 :]
    dense, channels, cells = own.shape
    planes, pair = dense // TB_DEV, CAP * channels
    labels = [row[planes * pair :, :].astype(jnp.float32) for row in rows]
    for m in range(planes):
        sums = [own[m * TB_DEV + k] for k in range(TB_DEV)]
        for row, label in zip(rows, labels):
            both = row[m * pair : (m + 1) * pair, :].astype(jnp.float32)
            for c in range(CAP):
                value = both[c * channels : (c + 1) * channels]
                mark = jnp.broadcast_to(label[m * CAP + c : m * CAP + c + 1], (channels, cells))
                sums = [s + jnp.where(mark == k, value, 0.0) for k, s in enumerate(sums)]
        for k, s in enumerate(sums):
            if len(outs) == 1:
                outs[0][(me[0] ^ m) * TB_DEV + k] = s.astype(outs[0].dtype)
            else:
                outs[m][k] = s.astype(outs[m].dtype)


def final_kernel(choose, weight, bias, *refs):
    *parts, remapped, embedded, turned = refs
    blocks, channels, cells = remapped.shape
    for b in range(blocks):
        value = sum(p[i + b].astype(jnp.float32) for p in parts for i in range(0, p.shape[0], blocks))
        value = value.astype(jnp.bfloat16)
        remapped[b] = value
        turned[b] = lax.dot_general(
            choose[...], value, (((1,), (1,)), ((), ())), preferred_element_type=jnp.float32
        )
    per_block = cells // (PATCH * PATCH)
    total = jnp.broadcast_to(bias[...], (blocks * per_block, bias.shape[1]))
    for s in range(PATCH * PATCH):
        rows = turned[:, s * per_block : (s + 1) * per_block, :]
        rows = rows.reshape(blocks * per_block, channels).astype(jnp.bfloat16)
        total = total + jnp.dot(rows, weight[s], preferred_element_type=jnp.float32)
    embedded[...] = total.astype(jnp.bfloat16)


def chooser(cells):
    per_block = cells // (PATCH * PATCH)
    row = jnp.arange(cells, dtype=jnp.int32)
    r, q, p = row // (PATCH * per_block), row // per_block % PATCH, row % per_block
    wanted = r * (PATCH * per_block) + p * PATCH + q
    return (wanted[:, None] == jnp.arange(cells, dtype=jnp.int32)[None, :]).astype(jnp.bfloat16)


def in_vmem(x):
    return pltpu.with_memory_space_constraint(x, pltpu.VMEM)


def in_hbm(x):
    return pltpu.with_memory_space_constraint(x, pltpu.HBM)


def limit(mib):
    return pltpu.CompilerParams(vmem_limit_bytes=mib << 20)


def local(
    source, tile_weight, tile_source, tile_slot, tile_count, dest_block, embed_weight, embed_bias
):
    channels, own_cells = source.shape
    tiles, block_size, _ = tile_weight.shape
    slots = dest_block.shape[0]
    peers = lax.axis_size("dom")
    me = lax.axis_index("dom").astype(jnp.int32)
    core = me & 1
    width = own_cells // 2
    emb = embed_weight.shape[1]
    members = 4 if peers == 16 else 2
    planes = peers // members

    def swap(x, q):
        return lax.ppermute(x, "dom", [(i, i ^ q) for i in range(peers)])

    near = swap(source, 1)
    far = lax.ppermute(
        lax.dynamic_slice_in_dim(source, core * width, width, axis=1),
        "dom",
        [(i, (i + (1 if i % 2 else -1)) % peers) for i in range(peers)],
    )

    by_swap = planes == 4
    spans = ((0, 2), (2, 4)) if by_swap else ((0, planes),)
    entries, segments = list_rows(tiles, slots)

    def table(rows):
        return jax.ShapeDtypeStruct((up(rows, 8), LANES), jnp.int32)

    def label_shape(lo, hi):
        return (members - 1, up((hi - lo) * CAP, 16), LANES)

    acc_shape = (slots, channels, block_size)
    list_table = table(entries + segments + 1)
    map_rows = up(planes * (TB_DEV + (members - 1) * CAP), LANES) // LANES
    flops = tiles * channels * block_size * block_size
    partial, held, late_list, *labels = pl.pallas_call(
        functools.partial(early_kernel, members, spans),
        out_shape=(
            pltpu.VMEM(acc_shape, jnp.float32),
            pltpu.VMEM((tiles + 1, block_size, block_size), jnp.bfloat16),
            table(entries + segments + 1 + map_rows),
            *[jax.ShapeDtypeStruct(label_shape(*span), jnp.bfloat16) for span in spans],
        ),
        in_specs=[SMEM, SMEM] + [ANY] * 6,
        out_specs=(VMEM,) * (3 + len(spans)),
        scratch_shapes=[
            pltpu.VMEM((channels, own_cells + width), jnp.bfloat16),
            pltpu.VMEM((2, 1, tiles), jnp.int32),
            pltpu.VMEM((1, slots), jnp.int32),
            pltpu.VMEM((2, *list_table.shape), jnp.int32),
            pltpu.SMEM(list_table.shape, jnp.int32),
            pltpu.SMEM(list_table.shape, jnp.int32),
            pltpu.SemaphoreType.DMA((7,)),
            pltpu.SemaphoreType.DMA((tiles // CHUNK,)),
        ],
        compiler_params=limit(8),
        cost_estimate=pl.CostEstimate(
            flops=2 * flops, bytes_accessed=tile_weight.size * 2, transcendentals=0
        ),
        name="early_tiles",
    )(
        me[None],
        tile_count,
        in_hbm(tile_source[None, :]),
        in_hbm(tile_slot[None, :]),
        in_hbm(dest_block[None, :]),
        in_hbm(source),
        near,
        in_hbm(tile_weight),
    )

    area = PATCH * PATCH
    weight = embed_weight.reshape(channels, area, emb).transpose(1, 0, 2)

    cells = (channels, block_size)
    part = (TB_DEV, *cells)
    late_shapes = []
    for (lo, hi), label in zip(spans, labels):
        row_total = (hi - lo) * CAP * channels + label.shape[1]
        late_shapes.append(pltpu.VMEM(((hi - lo) * TB_DEV, *cells), jnp.float32))
        late_shapes += [jax.ShapeDtypeStruct((row_total, block_size), jnp.bfloat16)] * (members - 1)
    late = pl.pallas_call(
        functools.partial(late_kernel, tiles, slots, members),
        out_shape=tuple(late_shapes),
        in_specs=[SMEM] + [VMEM] * (3 + len(labels)),
        out_specs=(VMEM,) * len(late_shapes),
        scratch_shapes=[pltpu.VMEM((slots + 1, *cells), jnp.float32)],
        compiler_params=limit(6),
        cost_estimate=pl.CostEstimate(
            flops=flops, bytes_accessed=2 * channels * width, transcendentals=0
        ),
        name="late_tiles",
    )(late_list, far, in_vmem(partial), in_vmem(held), *labels)
    own_rows = []
    for i in range(len(spans)):
        own, *rows = late[i * members : (i + 1) * members]
        own_rows.append((own, [swap(r, q + 1) for q, r in enumerate(rows)]))

    parts = []
    for (lo, hi), (own, rows) in zip(spans, own_rows):
        if by_swap:
            part_shapes = [
                jax.ShapeDtypeStruct(part, jnp.bfloat16) if m else pltpu.VMEM(part, jnp.float32)
                for m in range(lo, hi)
            ]
        else:
            part_shapes = [jax.ShapeDtypeStruct(own.shape, jnp.bfloat16)]
        sums = pl.pallas_call(
            functools.partial(plane_kernel, members),
            out_shape=tuple(part_shapes),
            in_specs=[SMEM] + [VMEM] * members,
            out_specs=(VMEM,) * len(part_shapes),
            compiler_params=limit(4),
            name="plane_sum",
        )((me // members)[None], in_vmem(own), *rows)
        if by_swap:
            parts += [swap(s, m * members) if m else s for m, s in zip(range(lo, hi), sums)]
        else:
            columns = [[z * members + i for z in range(planes)] for i in range(members)]
            parts.append(lax.all_to_all(sums[0], "dom", 0, 0, tiled=True, axis_index_groups=columns))

    per_block = block_size // area
    return pl.pallas_call(
        final_kernel,
        out_shape=(
            jax.ShapeDtypeStruct(part, jnp.bfloat16),
            jax.ShapeDtypeStruct((TB_DEV * per_block, emb), jnp.bfloat16),
        ),
        in_specs=[VMEM] * (3 + len(parts)),
        out_specs=(VMEM, VMEM),
        scratch_shapes=[pltpu.VMEM((TB_DEV, block_size, channels), jnp.float32)],
        compiler_params=limit(6),
        name="embed",
    )(chooser(block_size), weight, embed_bias.reshape(1, emb), *parts)


def solution(mesh):
    placed = (
        P(None, ("groups", "dom")),
        P("dom", None, None),
        P("dom"),
        P("dom"),
        P("dom"),
        P("dom"),
        P(),
        P(),
    )
    return jax.shard_map(
        local,
        mesh=mesh,
        in_specs=placed,
        out_specs=(P(("groups", "dom"), None, None), P(("groups", "dom"), None)),
        check_vma=False,
    )
```

```python
import functools

import jax
import jax.numpy as jnp
from jax import lax
from jax.experimental import pallas as pl
from jax.experimental.pallas import tpu as pltpu
from jax.sharding import PartitionSpec as P

PATCH = 4
CAP = 2
TB_DEV = 4
LANES = 128
SEG = 4
UNROLL = 20
CHUNK = 64
VMEM = pl.BlockSpec(memory_space=pltpu.VMEM)
SMEM = pl.BlockSpec(memory_space=pltpu.SMEM)
ANY = pl.BlockSpec(memory_space=pl.ANY)


def up(n, step):
    return -(-n // step) * step


def list_rows(tiles, slots):
    entries = up(up(tiles + slots * (SEG - 1), SEG * UNROLL), LANES) // LANES
    return entries, -(-entries // SEG)


def iota(shape, dim):
    return lax.broadcasted_iota(jnp.int32, shape, dim)


def ones_of(mask):
    return jnp.where(mask, 1.0, 0.0)


def dot(a, b, dims):
    return lax.dot_general(
        a.astype(jnp.bfloat16),
        b.astype(jnp.bfloat16),
        (dims, ((), ())),
        preferred_element_type=jnp.float32,
    )


def store_row(out, row, values):
    for r in range(values.shape[1] // LANES):
        out[row + r : row + r + 1, :] = values[:, r * LANES : (r + 1) * LANES]


def schedule(block, slot, kinds, slots, outs):
    tiles = block.shape[1]
    bits = tiles.bit_length()
    entries, segments = list_rows(tiles, slots)
    bins = len(kinds) * slots
    slot_is = slot == iota((slots, tiles), 0)
    chosen = jnp.concatenate([ones_of(slot_is & kind) for kind in kinds], axis=0)
    before = ones_of(iota((tiles, tiles), 0) < iota((tiles, tiles), 1))
    rank = dot(chosen, before, ((1,), (0,)))
    total = jnp.sum(chosen, axis=1, keepdims=True).astype(jnp.int32)
    length = jnp.broadcast_to((total + (SEG - 1)) // SEG, (bins, LANES))
    a, b = iota((bins, bins), 0), iota((bins, bins), 1)
    upto = ones_of((b <= a) & (b // slots == a // slots))
    ends = dot(upto, length.astype(jnp.float32), ((1,), (0,))).astype(jnp.int32)
    begins = (ends - length)[:, :1] * SEG + iota((bins, 1), 0) // slots * (entries * LANES)
    place = jnp.sum(chosen * (rank + begins.astype(jnp.float32) + 1.0), axis=0, keepdims=True)
    place = place.astype(jnp.int32) - 1
    rows = up(len(kinds) * entries, 8)
    at_row = ones_of((place >> 7) == iota((rows, tiles), 0))
    at_lane = ones_of((place & (LANES - 1)) == iota((LANES, tiles), 0))
    count = tiles - iota((1, tiles), 1)
    values = [at_row * v.astype(jnp.float32) for v in (block, count >> 5, count & 31)]
    found = dot(jnp.concatenate(values, axis=0), at_lane, ((1,), (1,))).astype(jnp.int32)
    code = (found[:rows] << bits) | (found[rows : 2 * rows] << 5) | found[2 * rows :]
    for k, out in enumerate(outs):
        mine = ends[k * slots : (k + 1) * slots]
        out[:entries, :] = code[k * entries : (k + 1) * entries]
        passed = ones_of(mine[:, :1] <= iota((slots, segments * LANES), 1))
        owner = jnp.sum(passed, axis=0, keepdims=True).astype(jnp.int32)
        store_row(out, entries, jnp.minimum(owner, slots - 1))
        out[entries + segments : entries + segments + 1, :] = mine[slots - 1 :]


def slot_places(dest, me, members):
    slots = dest.shape[1]
    a, b = iota((slots, slots), 0), iota((slots, slots), 1)
    column = jnp.sum(jnp.where(a == b, dest.astype(jnp.float32), 0.0), axis=1, keepdims=True)
    column = column.astype(jnp.int32)
    owner = column // TB_DEV
    earlier = ones_of((owner == dest // TB_DEV) & (b < a))
    rank = jnp.sum(earlier, axis=1, keepdims=True).astype(jnp.int32)
    return owner & (members - 1), (owner // members) ^ (me // members), rank, column & (TB_DEV - 1)


def run_segments(tiles, slots, meta, x, w, acc):
    entries, segments = list_rows(tiles, slots)
    bits = tiles.bit_length()
    total = meta[entries + segments, 0]

    def step(i, carry):
        results = []
        for u in range(UNROLL):
            first = (i * UNROLL + u) * SEG
            row, lane = first >> 7, first & (LANES - 1)
            xs, ws = [], []
            for k in range(SEG):
                code = meta[row, lane + k]
                column = pl.multiple_of((code >> bits) * LANES, LANES)
                xs.append(x[:, pl.ds(column, LANES)])
                ws.append(w[tiles - (code & ((1 << bits) - 1))])
            results.append(
                jnp.dot(
                    jnp.concatenate(xs, axis=1),
                    jnp.concatenate(ws, axis=0),
                    preferred_element_type=jnp.float32,
                )
            )
        for u in range(UNROLL):
            g = i * UNROLL + u
            slot = meta[entries + (g >> 7), g & (LANES - 1)]
            acc[slot] += results[u]
        return carry

    lax.fori_loop(0, (total + UNROLL - 1) // UNROLL, step, 0)


def early_kernel(members, spans, me, count, *refs):
    tile_source, tile_slot, dest, source, near, weights, acc, held, late_list, *refs = refs
    labels, (x, ids, dests, lists, meta_a, meta_b, sems, weight_sems) = refs[: len(spans)], refs[len(spans) :]
    tiles, slots = tile_source.shape[1], dest.shape[1]
    cells = source.shape[1]
    live, me, core = count[0], me[0], me[0] & 1
    chunks = tiles // CHUNK

    def copy(c):
        part = pl.ds(c * CHUNK, CHUNK)
        return pltpu.make_async_copy(weights.at[part], held.at[part], weight_sems.at[c])

    ids_in = [
        pltpu.make_async_copy(tile_source, ids.at[0], sems.at[0]),
        pltpu.make_async_copy(tile_slot, ids.at[1], sems.at[1]),
        pltpu.make_async_copy(dest, dests, sems.at[6]),
    ]
    for c in ids_in:
        c.start()
    for c in range(chunks):
        pl.when(c * CHUNK < live)(lambda c=c: copy(c).start())
    half = cells // 2
    first = pl.multiple_of(core * half, LANES)
    cells_in = [
        pltpu.make_async_copy(source, x.at[:, pl.ds(0, cells)], sems.at[2]),
        pltpu.make_async_copy(near.at[:, pl.ds(first, half)], x.at[:, pl.ds(cells, half)], sems.at[3]),
    ]
    for c in cells_in:
        c.start()
    for c in ids_in:
        c.wait()

    own = cells // LANES
    rim = own // 2
    place = ids[0]
    on_left, on_right = place < rim, place >= rim + own
    inner = ~(on_left | on_right)
    at_hand = inner | (on_left & (core == 1)) | (on_right & (core == 0))
    offset = jnp.where(on_right, place - own - rim, place)
    block = jnp.where(inner, place - rim, jnp.where(at_hand, own + offset, offset))
    tile_ids = iota((1, tiles), 1)
    alive = tile_ids < live
    member, plane, rank, block_row = slot_places(dests[...], me, members)
    member = member ^ (me & (members - 1))
    kinds = [alive & at_hand & (tile_ids < tiles // 2), alive & at_hand & (tile_ids >= tiles // 2)]
    kinds += [alive & ~at_hand]
    schedule(block, ids[1], kinds, slots, (lists.at[0], lists.at[1], late_list))
    to_scalars = [
        pltpu.make_async_copy(lists.at[0], meta_a, sems.at[4]),
        pltpu.make_async_copy(lists.at[1], meta_b, sems.at[5]),
    ]
    for c in to_scalars:
        c.start()

    entries, segments = list_rows(tiles, slots)
    first, goes = 0, jnp.zeros((slots, 1), jnp.int32)
    for (lo, hi), label in zip(spans, labels):
        dense, rows = (hi - lo) * TB_DEV, (hi - lo) * CAP
        inside = (plane >= lo) & (plane < hi)
        spot = (plane - lo) * CAP + rank
        place = jnp.where(member == 0, (plane - lo) * TB_DEV + block_row, dense + (member - 1) * rows + spot)
        goes = jnp.where(inside, first + place, goes)
        first += dense + (members - 1) * rows
        for q in range(1, members):
            hit = inside & (member == q) & (spot == iota((slots, label.shape[1]), 1))
            found = dot(ones_of(hit), jnp.broadcast_to(block_row + 1, (slots, LANES)), ((0,), (0,)))
            label[q - 1] = (found - 1.0).astype(label.dtype)
    hit = goes == iota((slots, up(first, LANES)), 1)
    sources = jnp.sum(jnp.where(hit, (iota((slots, 1), 0) - slots).astype(jnp.float32), 0.0), axis=0, keepdims=True)
    store_row(late_list, entries + segments + 1, sources.astype(jnp.int32) + slots)

    acc[...] = jnp.zeros_like(acc)
    held[tiles] = jnp.zeros(held.shape[1:], held.dtype)
    for c in (*cells_in, *to_scalars):
        c.wait()
    for part, meta in ((0, meta_a), (1, meta_b)):
        for c in range(part * chunks // 2, (part + 1) * chunks // 2):
            pl.when(c * CHUNK < live)(lambda c=c: copy(c).wait())
        run_segments(tiles, slots, meta, x, held, acc)


def late_kernel(tiles, slots, members, meta, far, partial, held, *rest):
    n = (len(rest) - 1) // (members + 1)
    labels, outs, acc = rest[:n], rest[n:-1], rest[-1]
    acc[:slots] = partial[...]
    acc[slots] = jnp.zeros(acc.shape[1:], acc.dtype)
    run_segments(tiles, slots, meta, far, held, acc)
    spot = sum(list_rows(tiles, slots)) + 1
    p = 0

    def next_slot():
        nonlocal p
        p += 1
        return acc[meta[spot + (p - 1) // LANES, (p - 1) % LANES]]

    for i, label in enumerate(labels):
        own, *rows = outs[i * members : (i + 1) * members]
        dense, pair = own.shape[0], CAP * own.shape[1]
        planes = dense // TB_DEV
        for r in range(dense):
            own[r] = next_slot()
        for q, out in enumerate(rows):
            for m in range(planes):
                both = jnp.concatenate([next_slot() for _ in range(CAP)], axis=0)
                out[m * pair : (m + 1) * pair, :] = both.astype(out.dtype)
            out[planes * pair :, :] = label[q]


def plane_kernel(members, me, own, *refs):
    rows, outs = refs[: members - 1], refs[members - 1 :]
    dense, channels, cells = own.shape
    planes, pair = dense // TB_DEV, CAP * channels
    labels = [row[planes * pair :, :].astype(jnp.float32) for row in rows]
    for m in range(planes):
        sums = [own[m * TB_DEV + k] for k in range(TB_DEV)]
        for row, label in zip(rows, labels):
            both = row[m * pair : (m + 1) * pair, :].astype(jnp.float32)
            for c in range(CAP):
                value = both[c * channels : (c + 1) * channels]
                mark = jnp.broadcast_to(label[m * CAP + c : m * CAP + c + 1], (channels, cells))
                sums = [s + jnp.where(mark == k, value, 0.0) for k, s in enumerate(sums)]
        for k, s in enumerate(sums):
            if len(outs) == 1:
                outs[0][(me[0] ^ m) * TB_DEV + k] = s.astype(outs[0].dtype)
            else:
                outs[m][k] = s.astype(outs[m].dtype)


def final_kernel(choose, weight, bias, *refs):
    *parts, remapped, embedded, turned = refs
    blocks, channels, cells = remapped.shape
    for b in range(blocks):
        value = sum(p[i + b].astype(jnp.float32) for p in parts for i in range(0, p.shape[0], blocks))
        value = value.astype(jnp.bfloat16)
        remapped[b] = value
        turned[b] = lax.dot_general(
            choose[...], value, (((1,), (1,)), ((), ())), preferred_element_type=jnp.float32
        )
    per_block = cells // (PATCH * PATCH)
    total = jnp.broadcast_to(bias[...], (blocks * per_block, bias.shape[1]))
    for s in range(PATCH * PATCH):
        rows = turned[:, s * per_block : (s + 1) * per_block, :]
        rows = rows.reshape(blocks * per_block, channels).astype(jnp.bfloat16)
        total = total + jnp.dot(rows, weight[s], preferred_element_type=jnp.float32)
    embedded[...] = total.astype(jnp.bfloat16)


def chooser(cells):
    per_block = cells // (PATCH * PATCH)
    row = jnp.arange(cells, dtype=jnp.int32)
    r, q, p = row // (PATCH * per_block), row // per_block % PATCH, row % per_block
    wanted = r * (PATCH * per_block) + p * PATCH + q
    return (wanted[:, None] == jnp.arange(cells, dtype=jnp.int32)[None, :]).astype(jnp.bfloat16)


def in_vmem(x):
    return pltpu.with_memory_space_constraint(x, pltpu.VMEM)


def in_hbm(x):
    return pltpu.with_memory_space_constraint(x, pltpu.HBM)


def limit(mib):
    return pltpu.CompilerParams(vmem_limit_bytes=mib << 20)


def local(
    source, tile_weight, tile_source, tile_slot, tile_count, dest_block, embed_weight, embed_bias
):
    channels, own_cells = source.shape
    tiles, block_size, _ = tile_weight.shape
    slots = dest_block.shape[0]
    peers = lax.axis_size("dom")
    me = lax.axis_index("dom").astype(jnp.int32)
    core = me & 1
    width = own_cells // 2
    emb = embed_weight.shape[1]
    members = 4 if peers == 16 else 2
    planes = peers // members

    def swap(x, q):
        return lax.ppermute(x, "dom", [(i, i ^ q) for i in range(peers)])

    near = swap(source, 1)
    far = lax.ppermute(
        lax.dynamic_slice_in_dim(source, core * width, width, axis=1),
        "dom",
        [(i, (i + (1 if i % 2 else -1)) % peers) for i in range(peers)],
    )

    by_swap = planes == 4
    spans = ((0, 2), (2, 4)) if by_swap else ((0, planes),)
    entries, segments = list_rows(tiles, slots)

    def table(rows):
        return jax.ShapeDtypeStruct((up(rows, 8), LANES), jnp.int32)

    def label_shape(lo, hi):
        return (members - 1, up((hi - lo) * CAP, 16), LANES)

    acc_shape = (slots, channels, block_size)
    list_table = table(entries + segments + 1)
    map_rows = up(planes * (TB_DEV + (members - 1) * CAP), LANES) // LANES
    flops = tiles * channels * block_size * block_size
    partial, held, late_list, *labels = pl.pallas_call(
        functools.partial(early_kernel, members, spans),
        out_shape=(
            pltpu.VMEM(acc_shape, jnp.float32),
            pltpu.VMEM((tiles + 1, block_size, block_size), jnp.bfloat16),
            table(entries + segments + 1 + map_rows),
            *[jax.ShapeDtypeStruct(label_shape(*span), jnp.bfloat16) for span in spans],
        ),
        in_specs=[SMEM, SMEM] + [ANY] * 6,
        out_specs=(VMEM,) * (3 + len(spans)),
        scratch_shapes=[
            pltpu.VMEM((channels, own_cells + width), jnp.bfloat16),
            pltpu.VMEM((2, 1, tiles), jnp.int32),
            pltpu.VMEM((1, slots), jnp.int32),
            pltpu.VMEM((2, *list_table.shape), jnp.int32),
            pltpu.SMEM(list_table.shape, jnp.int32),
            pltpu.SMEM(list_table.shape, jnp.int32),
            pltpu.SemaphoreType.DMA((7,)),
            pltpu.SemaphoreType.DMA((tiles // CHUNK,)),
        ],
        compiler_params=limit(8),
        cost_estimate=pl.CostEstimate(
            flops=2 * flops, bytes_accessed=tile_weight.size * 2, transcendentals=0
        ),
        name="early_tiles",
    )(
        me[None],
        tile_count,
        in_hbm(tile_source[None, :]),
        in_hbm(tile_slot[None, :]),
        in_hbm(dest_block[None, :]),
        in_hbm(source),
        near,
        in_hbm(tile_weight),
    )

    area = PATCH * PATCH
    weight = embed_weight.reshape(channels, area, emb).transpose(1, 0, 2)

    cells = (channels, block_size)
    part = (TB_DEV, *cells)
    late_shapes = []
    for (lo, hi), label in zip(spans, labels):
        row_total = (hi - lo) * CAP * channels + label.shape[1]
        late_shapes.append(pltpu.VMEM(((hi - lo) * TB_DEV, *cells), jnp.float32))
        late_shapes += [jax.ShapeDtypeStruct((row_total, block_size), jnp.bfloat16)] * (members - 1)
    late = pl.pallas_call(
        functools.partial(late_kernel, tiles, slots, members),
        out_shape=tuple(late_shapes),
        in_specs=[SMEM] + [VMEM] * (3 + len(labels)),
        out_specs=(VMEM,) * len(late_shapes),
        scratch_shapes=[pltpu.VMEM((slots + 1, *cells), jnp.float32)],
        compiler_params=limit(6),
        cost_estimate=pl.CostEstimate(
            flops=flops, bytes_accessed=2 * channels * width, transcendentals=0
        ),
        name="late_tiles",
    )(late_list, far, in_vmem(partial), in_vmem(held), *labels)
    own_rows = []
    for i in range(len(spans)):
        own, *rows = late[i * members : (i + 1) * members]
        swapped = [swap(r, q + 1) for q, r in enumerate(rows)]
        own_rows.append((own, swapped[1:] + swapped[:1]))

    parts = []
    for (lo, hi), (own, rows) in zip(spans, own_rows):
        if by_swap:
            part_shapes = [
                jax.ShapeDtypeStruct(part, jnp.bfloat16) if m else pltpu.VMEM(part, jnp.float32)
                for m in range(lo, hi)
            ]
        else:
            part_shapes = [jax.ShapeDtypeStruct(own.shape, jnp.bfloat16)]
        sums = pl.pallas_call(
            functools.partial(plane_kernel, members),
            out_shape=tuple(part_shapes),
            in_specs=[SMEM] + [VMEM] * members,
            out_specs=(VMEM,) * len(part_shapes),
            compiler_params=limit(4),
            name="plane_sum",
        )((me // members)[None], in_vmem(own), *rows)
        if by_swap:
            parts += [swap(s, m * members) if m else s for m, s in zip(range(lo, hi), sums)]
        else:
            columns = [[z * members + i for z in range(planes)] for i in range(members)]
            parts.append(lax.all_to_all(sums[0], "dom", 0, 0, tiled=True, axis_index_groups=columns))

    per_block = block_size // area
    return pl.pallas_call(
        final_kernel,
        out_shape=(
            jax.ShapeDtypeStruct(part, jnp.bfloat16),
            jax.ShapeDtypeStruct((TB_DEV * per_block, emb), jnp.bfloat16),
        ),
        in_specs=[VMEM] * (3 + len(parts)),
        out_specs=(VMEM, VMEM),
        scratch_shapes=[pltpu.VMEM((TB_DEV, block_size, channels), jnp.float32)],
        compiler_params=limit(6),
        name="embed",
    )(chooser(block_size), weight, embed_bias.reshape(1, emb), *parts)


def solution(mesh):
    placed = (
        P(None, ("groups", "dom")),
        P("dom", None, None),
        P("dom"),
        P("dom"),
        P("dom"),
        P("dom"),
        P(),
        P(),
    )
    return jax.shard_map(
        local,
        mesh=mesh,
        in_specs=placed,
        out_specs=(P(("groups", "dom"), None, None), P(("groups", "dom"), None)),
        check_vma=False,
    )
```

```python
import functools

import jax
import jax.numpy as jnp
from jax import lax
from jax.experimental import pallas as pl
from jax.experimental.pallas import tpu as pltpu
from jax.sharding import PartitionSpec as P

PATCH = 4
CAP = 2
TB_DEV = 4
LANES = 128
SEG = 4
UNROLL = 20
CHUNK = 64
VMEM = pl.BlockSpec(memory_space=pltpu.VMEM)
SMEM = pl.BlockSpec(memory_space=pltpu.SMEM)
ANY = pl.BlockSpec(memory_space=pl.ANY)


def up(n, step):
    return -(-n // step) * step


def list_rows(tiles, slots):
    entries = up(up(tiles + slots * (SEG - 1), SEG * UNROLL), LANES) // LANES
    return entries, -(-entries // SEG)


def iota(shape, dim):
    return lax.broadcasted_iota(jnp.int32, shape, dim)


def ones_of(mask):
    return jnp.where(mask, 1.0, 0.0)


def dot(a, b, dims):
    return lax.dot_general(
        a.astype(jnp.bfloat16),
        b.astype(jnp.bfloat16),
        (dims, ((), ())),
        preferred_element_type=jnp.float32,
    )


def store_row(out, row, values):
    for r in range(values.shape[1] // LANES):
        out[row + r : row + r + 1, :] = values[:, r * LANES : (r + 1) * LANES]


def schedule(block, slot, kinds, slots, outs):
    tiles = block.shape[1]
    bits = tiles.bit_length()
    entries, segments = list_rows(tiles, slots)
    bins = len(kinds) * slots
    slot_is = slot == iota((slots, tiles), 0)
    chosen = jnp.concatenate([ones_of(slot_is & kind) for kind in kinds], axis=0)
    before = ones_of(iota((tiles, tiles), 0) < iota((tiles, tiles), 1))
    rank = dot(chosen, before, ((1,), (0,)))
    total = jnp.sum(chosen, axis=1, keepdims=True).astype(jnp.int32)
    length = jnp.broadcast_to((total + (SEG - 1)) // SEG, (bins, LANES))
    a, b = iota((bins, bins), 0), iota((bins, bins), 1)
    upto = ones_of((b <= a) & (b // slots == a // slots))
    ends = dot(upto, length.astype(jnp.float32), ((1,), (0,))).astype(jnp.int32)
    begins = (ends - length)[:, :1] * SEG + iota((bins, 1), 0) // slots * (entries * LANES)
    place = jnp.sum(chosen * (rank + begins.astype(jnp.float32) + 1.0), axis=0, keepdims=True)
    place = place.astype(jnp.int32) - 1
    rows = up(len(kinds) * entries, 8)
    at_row = ones_of((place >> 7) == iota((rows, tiles), 0))
    at_lane = ones_of((place & (LANES - 1)) == iota((LANES, tiles), 0))
    count = tiles - iota((1, tiles), 1)
    values = [at_row * v.astype(jnp.float32) for v in (block, count >> 5, count & 31)]
    found = dot(jnp.concatenate(values, axis=0), at_lane, ((1,), (1,))).astype(jnp.int32)
    code = (found[:rows] << bits) | (found[rows : 2 * rows] << 5) | found[2 * rows :]
    for k, out in enumerate(outs):
        mine = ends[k * slots : (k + 1) * slots]
        out[:entries, :] = code[k * entries : (k + 1) * entries]
        passed = ones_of(mine[:, :1] <= iota((slots, segments * LANES), 1))
        owner = jnp.sum(passed, axis=0, keepdims=True).astype(jnp.int32)
        store_row(out, entries, jnp.minimum(owner, slots - 1))
        out[entries + segments : entries + segments + 1, :] = mine[slots - 1 :]


def slot_places(dest, me, members, planes):
    slots = dest.shape[1]
    a, b = iota((slots, slots), 0), iota((slots, slots), 1)
    column = jnp.sum(jnp.where(a == b, dest.astype(jnp.float32), 0.0), axis=1, keepdims=True)
    column = column.astype(jnp.int32)
    owner = column // TB_DEV
    earlier = ones_of((owner == dest // TB_DEV) & (b < a))
    rank = jnp.sum(earlier, axis=1, keepdims=True).astype(jnp.int32)
    plane = (owner // members - me // members + 1) & (planes - 1)
    return owner & (members - 1), plane, rank, column & (TB_DEV - 1)


def run_segments(tiles, slots, meta, x, w, acc):
    entries, segments = list_rows(tiles, slots)
    bits = tiles.bit_length()
    total = meta[entries + segments, 0]

    def step(i, carry):
        results = []
        for u in range(UNROLL):
            first = (i * UNROLL + u) * SEG
            row, lane = first >> 7, first & (LANES - 1)
            xs, ws = [], []
            for k in range(SEG):
                code = meta[row, lane + k]
                column = pl.multiple_of((code >> bits) * LANES, LANES)
                xs.append(x[:, pl.ds(column, LANES)])
                ws.append(w[tiles - (code & ((1 << bits) - 1))])
            results.append(
                jnp.dot(
                    jnp.concatenate(xs, axis=1),
                    jnp.concatenate(ws, axis=0),
                    preferred_element_type=jnp.float32,
                )
            )
        for u in range(UNROLL):
            g = i * UNROLL + u
            slot = meta[entries + (g >> 7), g & (LANES - 1)]
            acc[slot] += results[u]
        return carry

    lax.fori_loop(0, (total + UNROLL - 1) // UNROLL, step, 0)


def early_kernel(members, spans, me, count, *refs):
    tile_source, tile_slot, dest, source, near, weights, acc, held, late_list, *refs = refs
    labels, (x, ids, dests, lists, meta_a, meta_b, sems, weight_sems) = refs[: len(spans)], refs[len(spans) :]
    tiles, slots = tile_source.shape[1], dest.shape[1]
    cells = source.shape[1]
    live, me, core = count[0], me[0], me[0] & 1
    chunks = tiles // CHUNK

    def copy(c):
        part = pl.ds(c * CHUNK, CHUNK)
        return pltpu.make_async_copy(weights.at[part], held.at[part], weight_sems.at[c])

    ids_in = [
        pltpu.make_async_copy(tile_source, ids.at[0], sems.at[0]),
        pltpu.make_async_copy(tile_slot, ids.at[1], sems.at[1]),
        pltpu.make_async_copy(dest, dests, sems.at[6]),
    ]
    for c in ids_in:
        c.start()
    for c in range(chunks):
        pl.when(c * CHUNK < live)(lambda c=c: copy(c).start())
    half = cells // 2
    first = pl.multiple_of(core * half, LANES)
    cells_in = [
        pltpu.make_async_copy(source, x.at[:, pl.ds(0, cells)], sems.at[2]),
        pltpu.make_async_copy(near.at[:, pl.ds(first, half)], x.at[:, pl.ds(cells, half)], sems.at[3]),
    ]
    for c in cells_in:
        c.start()
    for c in ids_in:
        c.wait()

    own = cells // LANES
    rim = own // 2
    place = ids[0]
    on_left, on_right = place < rim, place >= rim + own
    inner = ~(on_left | on_right)
    at_hand = inner | (on_left & (core == 1)) | (on_right & (core == 0))
    offset = jnp.where(on_right, place - own - rim, place)
    block = jnp.where(inner, place - rim, jnp.where(at_hand, own + offset, offset))
    tile_ids = iota((1, tiles), 1)
    alive = tile_ids < live
    member, plane, rank, block_row = slot_places(dests[...], me, members, spans[-1][1])
    member = member ^ (me & (members - 1))
    kinds = [alive & at_hand & (tile_ids < tiles // 2), alive & at_hand & (tile_ids >= tiles // 2)]
    kinds += [alive & ~at_hand]
    schedule(block, ids[1], kinds, slots, (lists.at[0], lists.at[1], late_list))
    to_scalars = [
        pltpu.make_async_copy(lists.at[0], meta_a, sems.at[4]),
        pltpu.make_async_copy(lists.at[1], meta_b, sems.at[5]),
    ]
    for c in to_scalars:
        c.start()

    entries, segments = list_rows(tiles, slots)
    first, goes = 0, jnp.zeros((slots, 1), jnp.int32)
    for (lo, hi), label in zip(spans, labels):
        dense, rows = (hi - lo) * TB_DEV, (hi - lo) * CAP
        inside = (plane >= lo) & (plane < hi)
        spot = (plane - lo) * CAP + rank
        place = jnp.where(member == 0, (plane - lo) * TB_DEV + block_row, dense + (member - 1) * rows + spot)
        goes = jnp.where(inside, first + place, goes)
        first += dense + (members - 1) * rows
        for q in range(1, members):
            hit = inside & (member == q) & (spot == iota((slots, label.shape[1]), 1))
            found = dot(ones_of(hit), jnp.broadcast_to(block_row + 1, (slots, LANES)), ((0,), (0,)))
            label[q - 1] = (found - 1.0).astype(label.dtype)
    hit = goes == iota((slots, up(first, LANES)), 1)
    sources = jnp.sum(jnp.where(hit, (iota((slots, 1), 0) - slots).astype(jnp.float32), 0.0), axis=0, keepdims=True)
    store_row(late_list, entries + segments + 1, sources.astype(jnp.int32) + slots)

    acc[...] = jnp.zeros_like(acc)
    held[tiles] = jnp.zeros(held.shape[1:], held.dtype)
    for c in (*cells_in, *to_scalars):
        c.wait()
    for part, meta in ((0, meta_a), (1, meta_b)):
        for c in range(part * chunks // 2, (part + 1) * chunks // 2):
            pl.when(c * CHUNK < live)(lambda c=c: copy(c).wait())
        run_segments(tiles, slots, meta, x, held, acc)


def late_kernel(tiles, slots, members, meta, far, partial, held, *rest):
    n = (len(rest) - 1) // (members + 1)
    labels, outs, acc = rest[:n], rest[n:-1], rest[-1]
    acc[:slots] = partial[...]
    acc[slots] = jnp.zeros(acc.shape[1:], acc.dtype)
    run_segments(tiles, slots, meta, far, held, acc)
    spot = sum(list_rows(tiles, slots)) + 1
    p = 0

    def next_slot():
        nonlocal p
        p += 1
        return acc[meta[spot + (p - 1) // LANES, (p - 1) % LANES]]

    for i, label in enumerate(labels):
        own, *rows = outs[i * members : (i + 1) * members]
        dense, pair = own.shape[0], CAP * own.shape[1]
        planes = dense // TB_DEV
        for r in range(dense):
            own[r] = next_slot()
        for q, out in enumerate(rows):
            for m in range(planes):
                both = jnp.concatenate([next_slot() for _ in range(CAP)], axis=0)
                out[m * pair : (m + 1) * pair, :] = both.astype(out.dtype)
            out[planes * pair :, :] = label[q]


def plane_kernel(members, me, own, *refs):
    rows, outs = refs[: members - 1], refs[members - 1 :]
    dense, channels, cells = own.shape
    planes, pair = dense // TB_DEV, CAP * channels
    labels = [row[planes * pair :, :].astype(jnp.float32) for row in rows]
    for m in range(planes):
        sums = [own[m * TB_DEV + k] for k in range(TB_DEV)]
        for row, label in zip(rows, labels):
            both = row[m * pair : (m + 1) * pair, :].astype(jnp.float32)
            for c in range(CAP):
                value = both[c * channels : (c + 1) * channels]
                mark = jnp.broadcast_to(label[m * CAP + c : m * CAP + c + 1], (channels, cells))
                sums = [s + jnp.where(mark == k, value, 0.0) for k, s in enumerate(sums)]
        for k, s in enumerate(sums):
            if len(outs) == 1:
                outs[0][((me[0] + m - 1) & (planes - 1)) * TB_DEV + k] = s.astype(outs[0].dtype)
            else:
                outs[m][k] = s.astype(outs[m].dtype)


def final_kernel(choose, weight, bias, *refs):
    *parts, remapped, embedded, turned = refs
    blocks, channels, cells = remapped.shape
    for b in range(blocks):
        value = sum(p[i + b].astype(jnp.float32) for p in parts for i in range(0, p.shape[0], blocks))
        value = value.astype(jnp.bfloat16)
        remapped[b] = value
        turned[b] = lax.dot_general(
            choose[...], value, (((1,), (1,)), ((), ())), preferred_element_type=jnp.float32
        )
    per_block = cells // (PATCH * PATCH)
    total = jnp.broadcast_to(bias[...], (blocks * per_block, bias.shape[1]))
    for s in range(PATCH * PATCH):
        rows = turned[:, s * per_block : (s + 1) * per_block, :]
        rows = rows.reshape(blocks * per_block, channels).astype(jnp.bfloat16)
        total = total + jnp.dot(rows, weight[s], preferred_element_type=jnp.float32)
    embedded[...] = total.astype(jnp.bfloat16)


def chooser(cells):
    per_block = cells // (PATCH * PATCH)
    row = jnp.arange(cells, dtype=jnp.int32)
    r, q, p = row // (PATCH * per_block), row // per_block % PATCH, row % per_block
    wanted = r * (PATCH * per_block) + p * PATCH + q
    return (wanted[:, None] == jnp.arange(cells, dtype=jnp.int32)[None, :]).astype(jnp.bfloat16)


def in_vmem(x):
    return pltpu.with_memory_space_constraint(x, pltpu.VMEM)


def in_hbm(x):
    return pltpu.with_memory_space_constraint(x, pltpu.HBM)


def limit(mib):
    return pltpu.CompilerParams(vmem_limit_bytes=mib << 20)


def local(
    source, tile_weight, tile_source, tile_slot, tile_count, dest_block, embed_weight, embed_bias
):
    channels, own_cells = source.shape
    tiles, block_size, _ = tile_weight.shape
    slots = dest_block.shape[0]
    peers = lax.axis_size("dom")
    me = lax.axis_index("dom").astype(jnp.int32)
    core = me & 1
    width = own_cells // 2
    emb = embed_weight.shape[1]
    members = 4 if peers == 16 else 2
    planes = peers // members

    def swap(x, q):
        return lax.ppermute(x, "dom", [(i, i ^ q) for i in range(peers)])

    def shift(x, m):
        return lax.ppermute(x, "dom", [(i, (i + m * members) % peers) for i in range(peers)])

    near = swap(source, 1)
    far = lax.ppermute(
        lax.dynamic_slice_in_dim(source, core * width, width, axis=1),
        "dom",
        [(i, (i + (1 if i % 2 else -1)) % peers) for i in range(peers)],
    )

    by_swap = planes == 4
    spans = ((0, 2), (2, 4)) if by_swap else ((0, planes),)
    entries, segments = list_rows(tiles, slots)

    def table(rows):
        return jax.ShapeDtypeStruct((up(rows, 8), LANES), jnp.int32)

    def label_shape(lo, hi):
        return (members - 1, up((hi - lo) * CAP, 16), LANES)

    acc_shape = (slots, channels, block_size)
    list_table = table(entries + segments + 1)
    map_rows = up(planes * (TB_DEV + (members - 1) * CAP), LANES) // LANES
    flops = tiles * channels * block_size * block_size
    partial, held, late_list, *labels = pl.pallas_call(
        functools.partial(early_kernel, members, spans),
        out_shape=(
            pltpu.VMEM(acc_shape, jnp.float32),
            pltpu.VMEM((tiles + 1, block_size, block_size), jnp.bfloat16),
            table(entries + segments + 1 + map_rows),
            *[jax.ShapeDtypeStruct(label_shape(*span), jnp.bfloat16) for span in spans],
        ),
        in_specs=[SMEM, SMEM] + [ANY] * 6,
        out_specs=(VMEM,) * (3 + len(spans)),
        scratch_shapes=[
            pltpu.VMEM((channels, own_cells + width), jnp.bfloat16),
            pltpu.VMEM((2, 1, tiles), jnp.int32),
            pltpu.VMEM((1, slots), jnp.int32),
            pltpu.VMEM((2, *list_table.shape), jnp.int32),
            pltpu.SMEM(list_table.shape, jnp.int32),
            pltpu.SMEM(list_table.shape, jnp.int32),
            pltpu.SemaphoreType.DMA((7,)),
            pltpu.SemaphoreType.DMA((tiles // CHUNK,)),
        ],
        compiler_params=limit(8),
        cost_estimate=pl.CostEstimate(
            flops=2 * flops, bytes_accessed=tile_weight.size * 2, transcendentals=0
        ),
        name="early_tiles",
    )(
        me[None],
        tile_count,
        in_hbm(tile_source[None, :]),
        in_hbm(tile_slot[None, :]),
        in_hbm(dest_block[None, :]),
        in_hbm(source),
        near,
        in_hbm(tile_weight),
    )

    area = PATCH * PATCH
    weight = embed_weight.reshape(channels, area, emb).transpose(1, 0, 2)

    cells = (channels, block_size)
    part = (TB_DEV, *cells)
    late_shapes = []
    for (lo, hi), label in zip(spans, labels):
        row_total = (hi - lo) * CAP * channels + label.shape[1]
        late_shapes.append(pltpu.VMEM(((hi - lo) * TB_DEV, *cells), jnp.float32))
        late_shapes += [jax.ShapeDtypeStruct((row_total, block_size), jnp.bfloat16)] * (members - 1)
    late = pl.pallas_call(
        functools.partial(late_kernel, tiles, slots, members),
        out_shape=tuple(late_shapes),
        in_specs=[SMEM] + [VMEM] * (3 + len(labels)),
        out_specs=(VMEM,) * len(late_shapes),
        scratch_shapes=[pltpu.VMEM((slots + 1, *cells), jnp.float32)],
        compiler_params=limit(6),
        cost_estimate=pl.CostEstimate(
            flops=flops, bytes_accessed=2 * channels * width, transcendentals=0
        ),
        name="late_tiles",
    )(late_list, far, in_vmem(partial), in_vmem(held), *labels)
    own_rows = []
    for i in range(len(spans)):
        own, *rows = late[i * members : (i + 1) * members]
        swapped = [swap(r, q + 1) for q, r in enumerate(rows)]
        own_rows.append((own, swapped[1:] + swapped[:1]))

    parts = []
    for (lo, hi), (own, rows) in zip(spans, own_rows):
        if by_swap:
            part_shapes = [
                pltpu.VMEM(part, jnp.float32) if m == 1 else jax.ShapeDtypeStruct(part, jnp.bfloat16)
                for m in range(lo, hi)
            ]
        else:
            part_shapes = [jax.ShapeDtypeStruct(own.shape, jnp.bfloat16)]
        sums = pl.pallas_call(
            functools.partial(plane_kernel, members),
            out_shape=tuple(part_shapes),
            in_specs=[SMEM] + [VMEM] * members,
            out_specs=(VMEM,) * len(part_shapes),
            compiler_params=limit(4),
            name="plane_sum",
        )((me // members)[None], in_vmem(own), *rows)
        if by_swap:
            parts += [s if m == 1 else shift(s, m - 1) for m, s in zip(range(lo, hi), sums)][::-1]
        else:
            columns = [[z * members + i for z in range(planes)] for i in range(members)]
            parts.append(lax.all_to_all(sums[0], "dom", 0, 0, tiled=True, axis_index_groups=columns))

    per_block = block_size // area
    return pl.pallas_call(
        final_kernel,
        out_shape=(
            jax.ShapeDtypeStruct(part, jnp.bfloat16),
            jax.ShapeDtypeStruct((TB_DEV * per_block, emb), jnp.bfloat16),
        ),
        in_specs=[VMEM] * (3 + len(parts)),
        out_specs=(VMEM, VMEM),
        scratch_shapes=[pltpu.VMEM((TB_DEV, block_size, channels), jnp.float32)],
        compiler_params=limit(6),
        name="embed",
    )(chooser(block_size), weight, embed_bias.reshape(1, emb), *parts)


def solution(mesh):
    placed = (
        P(None, ("groups", "dom")),
        P("dom", None, None),
        P("dom"),
        P("dom"),
        P("dom"),
        P("dom"),
        P(),
        P(),
    )
    return jax.shard_map(
        local,
        mesh=mesh,
        in_specs=placed,
        out_specs=(P(("groups", "dom"), None, None), P(("groups", "dom"), None)),
        check_vma=False,
    )
```

```python
import functools

import jax
import jax.numpy as jnp
from jax import lax
from jax.experimental import pallas as pl
from jax.experimental.pallas import tpu as pltpu
from jax.sharding import PartitionSpec as P

PATCH = 4
CAP = 2
TB_DEV = 4
LANES = 128
SEG = 4
UNROLL = 20
CHUNK = 64
VMEM = pl.BlockSpec(memory_space=pltpu.VMEM)
SMEM = pl.BlockSpec(memory_space=pltpu.SMEM)
ANY = pl.BlockSpec(memory_space=pl.ANY)


def up(n, step):
    return -(-n // step) * step


def list_rows(tiles, slots):
    entries = up(up(tiles + slots * (SEG - 1), SEG * UNROLL), LANES) // LANES
    return entries, -(-entries // SEG)


def iota(shape, dim):
    return lax.broadcasted_iota(jnp.int32, shape, dim)


def ones_of(mask):
    return jnp.where(mask, 1.0, 0.0)


def dot(a, b, dims):
    return lax.dot_general(
        a.astype(jnp.bfloat16),
        b.astype(jnp.bfloat16),
        (dims, ((), ())),
        preferred_element_type=jnp.float32,
    )


def store_row(out, row, values):
    for r in range(values.shape[1] // LANES):
        out[row + r : row + r + 1, :] = values[:, r * LANES : (r + 1) * LANES]


def schedule(block, slot, kinds, slots, outs):
    tiles = block.shape[1]
    bits = tiles.bit_length()
    entries, segments = list_rows(tiles, slots)
    bins = len(kinds) * slots
    slot_is = slot == iota((slots, tiles), 0)
    chosen = jnp.concatenate([ones_of(slot_is & kind) for kind in kinds], axis=0)
    before = ones_of(iota((tiles, tiles), 0) < iota((tiles, tiles), 1))
    rank = dot(chosen, before, ((1,), (0,)))
    total = jnp.sum(chosen, axis=1, keepdims=True).astype(jnp.int32)
    length = jnp.broadcast_to((total + (SEG - 1)) // SEG, (bins, LANES))
    a, b = iota((bins, bins), 0), iota((bins, bins), 1)
    upto = ones_of((b <= a) & (b // slots == a // slots))
    ends = dot(upto, length.astype(jnp.float32), ((1,), (0,))).astype(jnp.int32)
    begins = (ends - length)[:, :1] * SEG + iota((bins, 1), 0) // slots * (entries * LANES)
    place = jnp.sum(chosen * (rank + begins.astype(jnp.float32) + 1.0), axis=0, keepdims=True)
    place = place.astype(jnp.int32) - 1
    rows = up(len(kinds) * entries, 8)
    at_row = ones_of((place >> 7) == iota((rows, tiles), 0))
    at_lane = ones_of((place & (LANES - 1)) == iota((LANES, tiles), 0))
    count = tiles - iota((1, tiles), 1)
    values = [at_row * v.astype(jnp.float32) for v in (block, count >> 5, count & 31)]
    found = dot(jnp.concatenate(values, axis=0), at_lane, ((1,), (1,))).astype(jnp.int32)
    code = (found[:rows] << bits) | (found[rows : 2 * rows] << 5) | found[2 * rows :]
    for k, out in enumerate(outs):
        mine = ends[k * slots : (k + 1) * slots]
        out[:entries, :] = code[k * entries : (k + 1) * entries]
        passed = ones_of(mine[:, :1] <= iota((slots, segments * LANES), 1))
        owner = jnp.sum(passed, axis=0, keepdims=True).astype(jnp.int32)
        store_row(out, entries, jnp.minimum(owner, slots - 1))
        out[entries + segments : entries + segments + 1, :] = mine[slots - 1 :]


def slot_places(dest, me, members, planes):
    slots = dest.shape[1]
    a, b = iota((slots, slots), 0), iota((slots, slots), 1)
    column = jnp.sum(jnp.where(a == b, dest.astype(jnp.float32), 0.0), axis=1, keepdims=True)
    column = column.astype(jnp.int32)
    owner = column // TB_DEV
    earlier = ones_of((owner == dest // TB_DEV) & (b < a))
    rank = jnp.sum(earlier, axis=1, keepdims=True).astype(jnp.int32)
    plane = (owner // members - me // members + 1) & (planes - 1)
    return owner & (members - 1), plane, rank, column & (TB_DEV - 1)


def run_segments(tiles, slots, meta, x, w, acc):
    entries, segments = list_rows(tiles, slots)
    bits = tiles.bit_length()
    total = meta[entries + segments, 0]

    def step(i, carry):
        results = []
        for u in range(UNROLL):
            first = (i * UNROLL + u) * SEG
            row, lane = first >> 7, first & (LANES - 1)
            xs, ws = [], []
            for k in range(SEG):
                code = meta[row, lane + k]
                column = pl.multiple_of((code >> bits) * LANES, LANES)
                xs.append(x[:, pl.ds(column, LANES)])
                ws.append(w[tiles - (code & ((1 << bits) - 1))])
            results.append(
                jnp.dot(
                    jnp.concatenate(xs, axis=1),
                    jnp.concatenate(ws, axis=0),
                    preferred_element_type=jnp.float32,
                )
            )
        for u in range(UNROLL):
            g = i * UNROLL + u
            slot = meta[entries + (g >> 7), g & (LANES - 1)]
            acc[slot] += results[u]
        return carry

    lax.fori_loop(0, (total + UNROLL - 1) // UNROLL, step, 0)


def early_kernel(members, spans, me, count, *refs):
    tile_source, tile_slot, dest, source, near, weights, acc, held, late_list, *refs = refs
    labels, (x, ids, dests, lists, meta_a, meta_b, sems, weight_sems) = refs[: len(spans)], refs[len(spans) :]
    tiles, slots = tile_source.shape[1], dest.shape[1]
    cells = source.shape[1]
    live, me, core = count[0], me[0], me[0] & 1
    chunks = tiles // CHUNK

    def copy(c):
        part = pl.ds(c * CHUNK, CHUNK)
        return pltpu.make_async_copy(weights.at[part], held.at[part], weight_sems.at[c])

    ids_in = [
        pltpu.make_async_copy(tile_source, ids.at[0], sems.at[0]),
        pltpu.make_async_copy(tile_slot, ids.at[1], sems.at[1]),
        pltpu.make_async_copy(dest, dests, sems.at[6]),
    ]
    for c in ids_in:
        c.start()
    for c in range(chunks):
        pl.when(c * CHUNK < live)(lambda c=c: copy(c).start())
    half = cells // 2
    first = pl.multiple_of(core * half, LANES)
    cells_in = [
        pltpu.make_async_copy(source, x.at[:, pl.ds(0, cells)], sems.at[2]),
        pltpu.make_async_copy(near.at[:, pl.ds(first, half)], x.at[:, pl.ds(cells, half)], sems.at[3]),
    ]
    for c in cells_in:
        c.start()
    for c in ids_in:
        c.wait()

    own = cells // LANES
    rim = own // 2
    place = ids[0]
    on_left, on_right = place < rim, place >= rim + own
    inner = ~(on_left | on_right)
    at_hand = inner | (on_left & (core == 1)) | (on_right & (core == 0))
    offset = jnp.where(on_right, place - own - rim, place)
    block = jnp.where(inner, place - rim, jnp.where(at_hand, own + offset, offset))
    tile_ids = iota((1, tiles), 1)
    alive = tile_ids < live
    member, plane, rank, block_row = slot_places(dests[...], me, members, spans[-1][1])
    member = member ^ (me & (members - 1))
    kinds = [alive & at_hand & (tile_ids < tiles // 2), alive & at_hand & (tile_ids >= tiles // 2)]
    kinds += [alive & ~at_hand]
    schedule(block, ids[1], kinds, slots, (lists.at[0], lists.at[1], late_list))
    to_scalars = [
        pltpu.make_async_copy(lists.at[0], meta_a, sems.at[4]),
        pltpu.make_async_copy(lists.at[1], meta_b, sems.at[5]),
    ]
    for c in to_scalars:
        c.start()

    entries, segments = list_rows(tiles, slots)
    first, goes = 0, jnp.zeros((slots, 1), jnp.int32)
    for (lo, hi), label in zip(spans, labels):
        dense, rows = (hi - lo) * TB_DEV, (hi - lo) * CAP
        inside = (plane >= lo) & (plane < hi)
        spot = (plane - lo) * CAP + rank
        place = jnp.where(member == 0, (plane - lo) * TB_DEV + block_row, dense + (member - 1) * rows + spot)
        goes = jnp.where(inside, first + place, goes)
        first += dense + (members - 1) * rows
        for q in range(1, members):
            hit = inside & (member == q) & (spot == iota((slots, label.shape[1]), 1))
            found = dot(ones_of(hit), jnp.broadcast_to(block_row + 1, (slots, LANES)), ((0,), (0,)))
            label[q - 1] = (found - 1.0).astype(label.dtype)
    hit = goes == iota((slots, up(first, LANES)), 1)
    sources = jnp.sum(jnp.where(hit, (iota((slots, 1), 0) - slots).astype(jnp.float32), 0.0), axis=0, keepdims=True)
    store_row(late_list, entries + segments + 1, sources.astype(jnp.int32) + slots)

    acc[...] = jnp.zeros_like(acc)
    held[tiles] = jnp.zeros(held.shape[1:], held.dtype)
    for c in (*cells_in, *to_scalars):
        c.wait()
    for part, meta in ((0, meta_a), (1, meta_b)):
        for c in range(part * chunks // 2, (part + 1) * chunks // 2):
            pl.when(c * CHUNK < live)(lambda c=c: copy(c).wait())
        run_segments(tiles, slots, meta, x, held, acc)


def late_kernel(tiles, slots, members, meta, far, partial, held, *rest):
    n = (len(rest) - 1) // (members + 1)
    labels, outs, acc = rest[:n], rest[n:-1], rest[-1]
    acc[:slots] = partial[...]
    acc[slots] = jnp.zeros(acc.shape[1:], acc.dtype)
    run_segments(tiles, slots, meta, far, held, acc)
    spot = sum(list_rows(tiles, slots)) + 1
    p = 0

    def next_slot():
        nonlocal p
        p += 1
        return acc[meta[spot + (p - 1) // LANES, (p - 1) % LANES]]

    for i, label in enumerate(labels):
        own, *rows = outs[i * members : (i + 1) * members]
        dense, pair = own.shape[0], CAP * own.shape[1]
        planes = dense // TB_DEV
        for r in range(dense):
            own[r] = next_slot()
        for q, out in enumerate(rows):
            for m in range(planes):
                both = jnp.concatenate([next_slot() for _ in range(CAP)], axis=0)
                out[m * pair : (m + 1) * pair, :] = both.astype(out.dtype)
            out[planes * pair :, :] = label[q]


def plane_kernel(members, me, own, *refs):
    rows, outs = refs[: members - 1], refs[members - 1 :]
    dense, channels, cells = own.shape
    planes, pair = dense // TB_DEV, CAP * channels
    labels = [row[planes * pair :, :].astype(jnp.float32) for row in rows]
    for m in range(planes):
        sums = [own[m * TB_DEV + k] for k in range(TB_DEV)]
        for row, label in zip(rows, labels):
            both = row[m * pair : (m + 1) * pair, :].astype(jnp.float32)
            for c in range(CAP):
                value = both[c * channels : (c + 1) * channels]
                mark = jnp.broadcast_to(label[m * CAP + c : m * CAP + c + 1], (channels, cells))
                sums = [s + jnp.where(mark == k, value, 0.0) for k, s in enumerate(sums)]
        for k, s in enumerate(sums):
            if len(outs) == 1:
                outs[0][((me[0] + m - 1) & (planes - 1)) * TB_DEV + k] = s.astype(outs[0].dtype)
            else:
                outs[m][k] = s.astype(outs[m].dtype)


def final_kernel(choose, weight, bias, *refs):
    *parts, remapped, embedded, turned = refs
    blocks, channels, cells = remapped.shape
    for b in range(blocks):
        value = sum(p[i + b].astype(jnp.float32) for p in parts for i in range(0, p.shape[0], blocks))
        value = value.astype(jnp.bfloat16)
        remapped[b] = value
        turned[b] = lax.dot_general(
            choose[...], value, (((1,), (1,)), ((), ())), preferred_element_type=jnp.float32
        )
    per_block = cells // (PATCH * PATCH)
    total = jnp.broadcast_to(bias[...], (blocks * per_block, bias.shape[1]))
    for s in range(PATCH * PATCH):
        rows = turned[:, s * per_block : (s + 1) * per_block, :]
        rows = rows.reshape(blocks * per_block, channels).astype(jnp.bfloat16)
        total = total + jnp.dot(rows, weight[s], preferred_element_type=jnp.float32)
    embedded[...] = total.astype(jnp.bfloat16)


def chooser(cells):
    per_block = cells // (PATCH * PATCH)
    row = jnp.arange(cells, dtype=jnp.int32)
    r, q, p = row // (PATCH * per_block), row // per_block % PATCH, row % per_block
    wanted = r * (PATCH * per_block) + p * PATCH + q
    return (wanted[:, None] == jnp.arange(cells, dtype=jnp.int32)[None, :]).astype(jnp.bfloat16)


def in_vmem(x):
    return pltpu.with_memory_space_constraint(x, pltpu.VMEM)


def in_hbm(x):
    return pltpu.with_memory_space_constraint(x, pltpu.HBM)


def limit(mib):
    return pltpu.CompilerParams(vmem_limit_bytes=mib << 20)


def local(
    source, tile_weight, tile_source, tile_slot, tile_count, dest_block, embed_weight, embed_bias
):
    channels, own_cells = source.shape
    tiles, block_size, _ = tile_weight.shape
    slots = dest_block.shape[0]
    peers = lax.axis_size("dom")
    me = lax.axis_index("dom").astype(jnp.int32)
    core = me & 1
    width = own_cells // 2
    emb = embed_weight.shape[1]
    members = 4 if peers == 16 else 2
    planes = peers // members

    def swap(x, q):
        return lax.ppermute(x, "dom", [(i, i ^ q) for i in range(peers)])

    def shift(x, m):
        return lax.ppermute(x, "dom", [(i, (i + m * members) % peers) for i in range(peers)])

    near = swap(source, 1)
    far = lax.ppermute(
        lax.dynamic_slice_in_dim(source, core * width, width, axis=1),
        "dom",
        [(i, (i + (1 if i % 2 else -1)) % peers) for i in range(peers)],
    )

    by_swap = planes == 4
    spans = ((0, 2), (2, 4)) if by_swap else ((0, planes),)
    entries, segments = list_rows(tiles, slots)

    def table(rows):
        return jax.ShapeDtypeStruct((up(rows, 8), LANES), jnp.int32)

    def label_shape(lo, hi):
        return (members - 1, up((hi - lo) * CAP, 16), LANES)

    acc_shape = (slots, channels, block_size)
    list_table = table(entries + segments + 1)
    map_rows = up(planes * (TB_DEV + (members - 1) * CAP), LANES) // LANES
    flops = tiles * channels * block_size * block_size
    partial, held, late_list, *labels = pl.pallas_call(
        functools.partial(early_kernel, members, spans),
        out_shape=(
            pltpu.VMEM(acc_shape, jnp.float32),
            pltpu.VMEM((tiles + 1, block_size, block_size), jnp.bfloat16),
            table(entries + segments + 1 + map_rows),
            *[jax.ShapeDtypeStruct(label_shape(*span), jnp.bfloat16) for span in spans],
        ),
        in_specs=[SMEM, SMEM] + [ANY] * 6,
        out_specs=(VMEM,) * (3 + len(spans)),
        scratch_shapes=[
            pltpu.VMEM((channels, own_cells + width), jnp.bfloat16),
            pltpu.VMEM((2, 1, tiles), jnp.int32),
            pltpu.VMEM((1, slots), jnp.int32),
            pltpu.VMEM((2, *list_table.shape), jnp.int32),
            pltpu.SMEM(list_table.shape, jnp.int32),
            pltpu.SMEM(list_table.shape, jnp.int32),
            pltpu.SemaphoreType.DMA((7,)),
            pltpu.SemaphoreType.DMA((tiles // CHUNK,)),
        ],
        compiler_params=limit(8),
        cost_estimate=pl.CostEstimate(
            flops=2 * flops, bytes_accessed=tile_weight.size * 2, transcendentals=0
        ),
        name="early_tiles",
    )(
        me[None],
        tile_count,
        in_hbm(tile_source[None, :]),
        in_hbm(tile_slot[None, :]),
        in_hbm(dest_block[None, :]),
        in_hbm(source),
        near,
        in_hbm(tile_weight),
    )

    area = PATCH * PATCH
    weight = embed_weight.reshape(channels, area, emb).transpose(1, 0, 2)

    cells = (channels, block_size)
    part = (TB_DEV, *cells)
    late_shapes = []
    for (lo, hi), label in zip(spans, labels):
        row_total = (hi - lo) * CAP * channels + label.shape[1]
        late_shapes.append(pltpu.VMEM(((hi - lo) * TB_DEV, *cells), jnp.float32))
        late_shapes += [jax.ShapeDtypeStruct((row_total, block_size), jnp.bfloat16)] * (members - 1)
    late = pl.pallas_call(
        functools.partial(late_kernel, tiles, slots, members),
        out_shape=tuple(late_shapes),
        in_specs=[SMEM] + [VMEM] * (3 + len(labels)),
        out_specs=(VMEM,) * len(late_shapes),
        scratch_shapes=[pltpu.VMEM((slots + 1, *cells), jnp.float32)],
        compiler_params=limit(6),
        cost_estimate=pl.CostEstimate(
            flops=flops, bytes_accessed=2 * channels * width, transcendentals=0
        ),
        name="late_tiles",
    )(late_list, far, in_vmem(partial), in_vmem(held), *labels)
    own_rows = []
    for i in range(len(spans)):
        own, *rows = late[i * members : (i + 1) * members]
        swapped = [swap(r, q + 1) for q, r in enumerate(rows)]
        own_rows.append((own, swapped[::-1]))

    parts = []
    for (lo, hi), (own, rows) in zip(spans, own_rows):
        if by_swap:
            part_shapes = [
                pltpu.VMEM(part, jnp.float32) if m == 1 else jax.ShapeDtypeStruct(part, jnp.bfloat16)
                for m in range(lo, hi)
            ]
        else:
            part_shapes = [jax.ShapeDtypeStruct(own.shape, jnp.bfloat16)]
        sums = pl.pallas_call(
            functools.partial(plane_kernel, members),
            out_shape=tuple(part_shapes),
            in_specs=[SMEM] + [VMEM] * members,
            out_specs=(VMEM,) * len(part_shapes),
            compiler_params=limit(4),
            name="plane_sum",
        )((me // members)[None], in_vmem(own), *rows)
        if by_swap:
            parts += [s if m == 1 else shift(s, m - 1) for m, s in zip(range(lo, hi), sums)][::-1]
        else:
            columns = [[z * members + i for z in range(planes)] for i in range(members)]
            parts.append(lax.all_to_all(sums[0], "dom", 0, 0, tiled=True, axis_index_groups=columns))

    per_block = block_size // area
    return pl.pallas_call(
        final_kernel,
        out_shape=(
            jax.ShapeDtypeStruct(part, jnp.bfloat16),
            jax.ShapeDtypeStruct((TB_DEV * per_block, emb), jnp.bfloat16),
        ),
        in_specs=[VMEM] * (3 + len(parts)),
        out_specs=(VMEM, VMEM),
        scratch_shapes=[pltpu.VMEM((TB_DEV, block_size, channels), jnp.float32)],
        compiler_params=limit(6),
        name="embed",
    )(chooser(block_size), weight, embed_bias.reshape(1, emb), *parts)


def solution(mesh):
    placed = (
        P(None, ("groups", "dom")),
        P("dom", None, None),
        P("dom"),
        P("dom"),
        P("dom"),
        P("dom"),
        P(),
        P(),
    )
    return jax.shard_map(
        local,
        mesh=mesh,
        in_specs=placed,
        out_specs=(P(("groups", "dom"), None, None), P(("groups", "dom"), None)),
        check_vma=False,
    )
```

```python
import functools

import jax
import jax.numpy as jnp
from jax import lax
from jax.experimental import pallas as pl
from jax.experimental.pallas import tpu as pltpu
from jax.sharding import PartitionSpec as P

PATCH = 4
CAP = 2
TB_DEV = 4
LANES = 128
SEG = 4
UNROLL = 20
CHUNK = 64
VMEM = pl.BlockSpec(memory_space=pltpu.VMEM)
SMEM = pl.BlockSpec(memory_space=pltpu.SMEM)
ANY = pl.BlockSpec(memory_space=pl.ANY)


def up(n, step):
    return -(-n // step) * step


def list_rows(tiles, slots):
    entries = up(up(tiles + slots * (SEG - 1), SEG * UNROLL), LANES) // LANES
    return entries, -(-entries // SEG)


def iota(shape, dim):
    return lax.broadcasted_iota(jnp.int32, shape, dim)


def ones_of(mask):
    return jnp.where(mask, 1.0, 0.0)


def dot(a, b, dims):
    return lax.dot_general(
        a.astype(jnp.bfloat16),
        b.astype(jnp.bfloat16),
        (dims, ((), ())),
        preferred_element_type=jnp.float32,
    )


def store_row(out, row, values):
    for r in range(values.shape[1] // LANES):
        out[row + r : row + r + 1, :] = values[:, r * LANES : (r + 1) * LANES]


def schedule(block, slot, kinds, slots, outs):
    tiles = block.shape[1]
    bits = tiles.bit_length()
    entries, segments = list_rows(tiles, slots)
    bins = len(kinds) * slots
    slot_is = slot == iota((slots, tiles), 0)
    chosen = jnp.concatenate([ones_of(slot_is & kind) for kind in kinds], axis=0)
    before = ones_of(iota((tiles, tiles), 0) < iota((tiles, tiles), 1))
    rank = dot(chosen, before, ((1,), (0,)))
    total = jnp.sum(chosen, axis=1, keepdims=True).astype(jnp.int32)
    length = jnp.broadcast_to((total + (SEG - 1)) // SEG, (bins, LANES))
    a, b = iota((bins, bins), 0), iota((bins, bins), 1)
    upto = ones_of((b <= a) & (b // slots == a // slots))
    ends = dot(upto, length.astype(jnp.float32), ((1,), (0,))).astype(jnp.int32)
    begins = (ends - length)[:, :1] * SEG + iota((bins, 1), 0) // slots * (entries * LANES)
    place = jnp.sum(chosen * (rank + begins.astype(jnp.float32) + 1.0), axis=0, keepdims=True)
    place = place.astype(jnp.int32) - 1
    rows = up(len(kinds) * entries, 8)
    at_row = ones_of((place >> 7) == iota((rows, tiles), 0))
    at_lane = ones_of((place & (LANES - 1)) == iota((LANES, tiles), 0))
    count = tiles - iota((1, tiles), 1)
    values = [at_row * v.astype(jnp.float32) for v in (block, count >> 5, count & 31)]
    found = dot(jnp.concatenate(values, axis=0), at_lane, ((1,), (1,))).astype(jnp.int32)
    code = (found[:rows] << bits) | (found[rows : 2 * rows] << 5) | found[2 * rows :]
    for k, out in enumerate(outs):
        mine = ends[k * slots : (k + 1) * slots]
        out[:entries, :] = code[k * entries : (k + 1) * entries]
        passed = ones_of(mine[:, :1] <= iota((slots, segments * LANES), 1))
        owner = jnp.sum(passed, axis=0, keepdims=True).astype(jnp.int32)
        store_row(out, entries, jnp.minimum(owner, slots - 1))
        out[entries + segments : entries + segments + 1, :] = mine[slots - 1 :]


def slot_places(dest, me, members, planes):
    slots = dest.shape[1]
    a, b = iota((slots, slots), 0), iota((slots, slots), 1)
    column = jnp.sum(jnp.where(a == b, dest.astype(jnp.float32), 0.0), axis=1, keepdims=True)
    column = column.astype(jnp.int32)
    owner = column // TB_DEV
    earlier = ones_of((owner == dest // TB_DEV) & (b < a))
    rank = jnp.sum(earlier, axis=1, keepdims=True).astype(jnp.int32)
    plane = (owner // members - me // members + 1) & (planes - 1)
    return owner & (members - 1), plane, rank, column & (TB_DEV - 1)


def run_segments(tiles, slots, meta, x, w, acc):
    entries, segments = list_rows(tiles, slots)
    bits = tiles.bit_length()
    total = meta[entries + segments, 0]

    def step(i, carry):
        results = []
        for u in range(UNROLL):
            first = (i * UNROLL + u) * SEG
            row, lane = first >> 7, first & (LANES - 1)
            xs, ws = [], []
            for k in range(SEG):
                code = meta[row, lane + k]
                column = pl.multiple_of((code >> bits) * LANES, LANES)
                xs.append(x[:, pl.ds(column, LANES)])
                ws.append(w[tiles - (code & ((1 << bits) - 1))])
            results.append(
                jnp.dot(
                    jnp.concatenate(xs, axis=1),
                    jnp.concatenate(ws, axis=0),
                    preferred_element_type=jnp.float32,
                )
            )
        for u in range(UNROLL):
            g = i * UNROLL + u
            slot = meta[entries + (g >> 7), g & (LANES - 1)]
            acc[slot] += results[u]
        return carry

    lax.fori_loop(0, (total + UNROLL - 1) // UNROLL, step, 0)


def early_kernel(members, spans, me, count, *refs):
    tile_source, tile_slot, dest, source, near, weights, acc, held, late_list, *refs = refs
    labels, (x, ids, dests, lists, meta_a, meta_b, sems, weight_sems) = refs[: len(spans)], refs[len(spans) :]
    tiles, slots = tile_source.shape[1], dest.shape[1]
    cells = source.shape[1]
    live, me, core = count[0], me[0], me[0] & 1
    chunks = tiles // CHUNK

    def copy(c):
        part = pl.ds(c * CHUNK, CHUNK)
        return pltpu.make_async_copy(weights.at[part], held.at[part], weight_sems.at[c])

    ids_in = [
        pltpu.make_async_copy(tile_source, ids.at[0], sems.at[0]),
        pltpu.make_async_copy(tile_slot, ids.at[1], sems.at[1]),
        pltpu.make_async_copy(dest, dests, sems.at[6]),
    ]
    for c in ids_in:
        c.start()
    for c in range(chunks):
        pl.when(c * CHUNK < live)(lambda c=c: copy(c).start())
    half = cells // 2
    first = pl.multiple_of(core * half, LANES)
    cells_in = [
        pltpu.make_async_copy(source, x.at[:, pl.ds(0, cells)], sems.at[2]),
        pltpu.make_async_copy(near.at[:, pl.ds(first, half)], x.at[:, pl.ds(cells, half)], sems.at[3]),
    ]
    for c in cells_in:
        c.start()
    for c in ids_in:
        c.wait()

    own = cells // LANES
    rim = own // 2
    place = ids[0]
    on_left, on_right = place < rim, place >= rim + own
    inner = ~(on_left | on_right)
    at_hand = inner | (on_left & (core == 1)) | (on_right & (core == 0))
    offset = jnp.where(on_right, place - own - rim, place)
    block = jnp.where(inner, place - rim, jnp.where(at_hand, own + offset, offset))
    tile_ids = iota((1, tiles), 1)
    alive = tile_ids < live
    member, plane, rank, block_row = slot_places(dests[...], me, members, spans[-1][1])
    member = member ^ (me & (members - 1))
    kinds = [alive & at_hand & (tile_ids < tiles // 2), alive & at_hand & (tile_ids >= tiles // 2)]
    kinds += [alive & ~at_hand]
    schedule(block, ids[1], kinds, slots, (lists.at[0], lists.at[1], late_list))
    to_scalars = [
        pltpu.make_async_copy(lists.at[0], meta_a, sems.at[4]),
        pltpu.make_async_copy(lists.at[1], meta_b, sems.at[5]),
    ]
    for c in to_scalars:
        c.start()

    entries, segments = list_rows(tiles, slots)
    first, goes = 0, jnp.zeros((slots, 1), jnp.int32)
    for (lo, hi), label in zip(spans, labels):
        dense, rows = (hi - lo) * TB_DEV, (hi - lo) * CAP
        inside = (plane >= lo) & (plane < hi)
        spot = (plane - lo) * CAP + rank
        place = jnp.where(member == 0, (plane - lo) * TB_DEV + block_row, dense + (member - 1) * rows + spot)
        goes = jnp.where(inside, first + place, goes)
        first += dense + (members - 1) * rows
        for q in range(1, members):
            hit = inside & (member == q) & (spot == iota((slots, label.shape[1]), 1))
            found = dot(ones_of(hit), jnp.broadcast_to(block_row + 1, (slots, LANES)), ((0,), (0,)))
            label[q - 1] = (found - 1.0).astype(label.dtype)
    hit = goes == iota((slots, up(first, LANES)), 1)
    sources = jnp.sum(jnp.where(hit, (iota((slots, 1), 0) - slots).astype(jnp.float32), 0.0), axis=0, keepdims=True)
    store_row(late_list, entries + segments + 1, sources.astype(jnp.int32) + slots)

    acc[...] = jnp.zeros_like(acc)
    held[tiles] = jnp.zeros(held.shape[1:], held.dtype)
    for c in (*cells_in, *to_scalars):
        c.wait()
    for part, meta in ((0, meta_a), (1, meta_b)):
        for c in range(part * chunks // 2, (part + 1) * chunks // 2):
            pl.when(c * CHUNK < live)(lambda c=c: copy(c).wait())
        run_segments(tiles, slots, meta, x, held, acc)


def late_kernel(tiles, slots, members, meta, far, partial, held, *rest):
    n = (len(rest) - 1) // (members + 1)
    labels, outs, acc = rest[:n], rest[n:-1], rest[-1]
    acc[:slots] = partial[...]
    run_segments(tiles, slots, meta, far, held, acc)
    acc[slots] = jnp.zeros(acc.shape[1:], acc.dtype)
    spot = sum(list_rows(tiles, slots)) + 1
    p = 0

    def next_slot():
        nonlocal p
        p += 1
        return acc[meta[spot + (p - 1) // LANES, (p - 1) % LANES]]

    for i, label in enumerate(labels):
        own, *rows = outs[i * members : (i + 1) * members]
        dense, pair = own.shape[0], CAP * own.shape[1]
        planes = dense // TB_DEV
        for r in range(dense):
            own[r] = next_slot()
        for q, out in enumerate(rows):
            for m in range(planes):
                both = jnp.concatenate([next_slot() for _ in range(CAP)], axis=0)
                out[m * pair : (m + 1) * pair, :] = both.astype(out.dtype)
            out[planes * pair :, :] = label[q]


def plane_kernel(members, me, own, *refs):
    rows, outs = refs[: members - 1], refs[members - 1 :]
    dense, channels, cells = own.shape
    planes, pair = dense // TB_DEV, CAP * channels
    labels = [row[planes * pair :, :].astype(jnp.float32) for row in rows]
    for m in range(planes):
        sums = [own[m * TB_DEV + k] for k in range(TB_DEV)]
        for row, label in zip(rows, labels):
            both = row[m * pair : (m + 1) * pair, :].astype(jnp.float32)
            for c in range(CAP):
                value = both[c * channels : (c + 1) * channels]
                mark = jnp.broadcast_to(label[m * CAP + c : m * CAP + c + 1], (channels, cells))
                sums = [s + jnp.where(mark == k, value, 0.0) for k, s in enumerate(sums)]
        for k, s in enumerate(sums):
            if len(outs) == 1:
                outs[0][((me[0] + m - 1) & (planes - 1)) * TB_DEV + k] = s.astype(outs[0].dtype)
            else:
                outs[m][k] = s.astype(outs[m].dtype)


def final_kernel(choose, weight, bias, *refs):
    *parts, remapped, embedded, turned = refs
    blocks, channels, cells = remapped.shape
    for b in range(blocks):
        value = sum(p[i + b].astype(jnp.float32) for p in parts for i in range(0, p.shape[0], blocks))
        value = value.astype(jnp.bfloat16)
        remapped[b] = value
        turned[b] = lax.dot_general(
            choose[...], value, (((1,), (1,)), ((), ())), preferred_element_type=jnp.float32
        )
    per_block = cells // (PATCH * PATCH)
    total = jnp.broadcast_to(bias[...], (blocks * per_block, bias.shape[1]))
    for s in range(PATCH * PATCH):
        rows = turned[:, s * per_block : (s + 1) * per_block, :]
        rows = rows.reshape(blocks * per_block, channels).astype(jnp.bfloat16)
        total = total + jnp.dot(rows, weight[s], preferred_element_type=jnp.float32)
    embedded[...] = total.astype(jnp.bfloat16)


def chooser(cells):
    per_block = cells // (PATCH * PATCH)
    row = jnp.arange(cells, dtype=jnp.int32)
    r, q, p = row // (PATCH * per_block), row // per_block % PATCH, row % per_block
    wanted = r * (PATCH * per_block) + p * PATCH + q
    return (wanted[:, None] == jnp.arange(cells, dtype=jnp.int32)[None, :]).astype(jnp.bfloat16)


def in_vmem(x):
    return pltpu.with_memory_space_constraint(x, pltpu.VMEM)


def in_hbm(x):
    return pltpu.with_memory_space_constraint(x, pltpu.HBM)


def limit(mib):
    return pltpu.CompilerParams(vmem_limit_bytes=mib << 20)


def local(
    source, tile_weight, tile_source, tile_slot, tile_count, dest_block, embed_weight, embed_bias
):
    channels, own_cells = source.shape
    tiles, block_size, _ = tile_weight.shape
    slots = dest_block.shape[0]
    peers = lax.axis_size("dom")
    me = lax.axis_index("dom").astype(jnp.int32)
    core = me & 1
    width = own_cells // 2
    emb = embed_weight.shape[1]
    members = 4 if peers == 16 else 2
    planes = peers // members

    def swap(x, q):
        return lax.ppermute(x, "dom", [(i, i ^ q) for i in range(peers)])

    def shift(x, m):
        return lax.ppermute(x, "dom", [(i, (i + m * members) % peers) for i in range(peers)])

    near = swap(source, 1)
    far = lax.ppermute(
        lax.dynamic_slice_in_dim(source, core * width, width, axis=1),
        "dom",
        [(i, (i + (1 if i % 2 else -1)) % peers) for i in range(peers)],
    )

    by_swap = planes == 4
    spans = ((0, 2), (2, 4)) if by_swap else ((0, planes),)
    entries, segments = list_rows(tiles, slots)

    def table(rows):
        return jax.ShapeDtypeStruct((up(rows, 8), LANES), jnp.int32)

    def label_shape(lo, hi):
        return (members - 1, up((hi - lo) * CAP, 16), LANES)

    acc_shape = (slots, channels, block_size)
    list_table = table(entries + segments + 1)
    map_rows = up(planes * (TB_DEV + (members - 1) * CAP), LANES) // LANES
    flops = tiles * channels * block_size * block_size
    partial, held, late_list, *labels = pl.pallas_call(
        functools.partial(early_kernel, members, spans),
        out_shape=(
            pltpu.VMEM(acc_shape, jnp.float32),
            pltpu.VMEM((tiles + 1, block_size, block_size), jnp.bfloat16),
            table(entries + segments + 1 + map_rows),
            *[jax.ShapeDtypeStruct(label_shape(*span), jnp.bfloat16) for span in spans],
        ),
        in_specs=[SMEM, SMEM] + [ANY] * 6,
        out_specs=(VMEM,) * (3 + len(spans)),
        scratch_shapes=[
            pltpu.VMEM((channels, own_cells + width), jnp.bfloat16),
            pltpu.VMEM((2, 1, tiles), jnp.int32),
            pltpu.VMEM((1, slots), jnp.int32),
            pltpu.VMEM((2, *list_table.shape), jnp.int32),
            pltpu.SMEM(list_table.shape, jnp.int32),
            pltpu.SMEM(list_table.shape, jnp.int32),
            pltpu.SemaphoreType.DMA((7,)),
            pltpu.SemaphoreType.DMA((tiles // CHUNK,)),
        ],
        compiler_params=limit(8),
        cost_estimate=pl.CostEstimate(
            flops=2 * flops, bytes_accessed=tile_weight.size * 2, transcendentals=0
        ),
        name="early_tiles",
    )(
        me[None],
        tile_count,
        in_hbm(tile_source[None, :]),
        in_hbm(tile_slot[None, :]),
        in_hbm(dest_block[None, :]),
        in_hbm(source),
        near,
        in_hbm(tile_weight),
    )

    area = PATCH * PATCH
    weight = embed_weight.reshape(channels, area, emb).transpose(1, 0, 2)

    cells = (channels, block_size)
    part = (TB_DEV, *cells)
    late_shapes = []
    for (lo, hi), label in zip(spans, labels):
        row_total = (hi - lo) * CAP * channels + label.shape[1]
        late_shapes.append(pltpu.VMEM(((hi - lo) * TB_DEV, *cells), jnp.float32))
        late_shapes += [jax.ShapeDtypeStruct((row_total, block_size), jnp.bfloat16)] * (members - 1)
    late = pl.pallas_call(
        functools.partial(late_kernel, tiles, slots, members),
        out_shape=tuple(late_shapes),
        in_specs=[SMEM] + [VMEM] * (3 + len(labels)),
        out_specs=(VMEM,) * len(late_shapes),
        scratch_shapes=[pltpu.VMEM((slots + 1, *cells), jnp.float32)],
        compiler_params=limit(6),
        cost_estimate=pl.CostEstimate(
            flops=flops, bytes_accessed=2 * channels * width, transcendentals=0
        ),
        name="late_tiles",
    )(late_list, far, in_vmem(partial), in_vmem(held), *labels)
    own_rows = []
    for i in range(len(spans)):
        own, *rows = late[i * members : (i + 1) * members]
        swapped = [swap(r, q + 1) for q, r in enumerate(rows)]
        own_rows.append((own, swapped[1:] + swapped[:1]))

    parts = []
    for (lo, hi), (own, rows) in zip(spans, own_rows):
        if by_swap:
            part_shapes = [
                pltpu.VMEM(part, jnp.float32) if m == 1 else jax.ShapeDtypeStruct(part, jnp.bfloat16)
                for m in range(lo, hi)
            ]
        else:
            part_shapes = [jax.ShapeDtypeStruct(own.shape, jnp.bfloat16)]
        sums = pl.pallas_call(
            functools.partial(plane_kernel, members),
            out_shape=tuple(part_shapes),
            in_specs=[SMEM] + [VMEM] * members,
            out_specs=(VMEM,) * len(part_shapes),
            compiler_params=limit(4),
            name="plane_sum",
        )((me // members)[None], in_vmem(own), *rows)
        if by_swap:
            parts += [s if m == 1 else shift(s, m - 1) for m, s in zip(range(lo, hi), sums)][::-1]
        else:
            columns = [[z * members + i for z in range(planes)] for i in range(members)]
            parts.append(lax.all_to_all(sums[0], "dom", 0, 0, tiled=True, axis_index_groups=columns))

    per_block = block_size // area
    return pl.pallas_call(
        final_kernel,
        out_shape=(
            jax.ShapeDtypeStruct(part, jnp.bfloat16),
            jax.ShapeDtypeStruct((TB_DEV * per_block, emb), jnp.bfloat16),
        ),
        in_specs=[VMEM] * (3 + len(parts)),
        out_specs=(VMEM, VMEM),
        scratch_shapes=[pltpu.VMEM((TB_DEV, block_size, channels), jnp.float32)],
        compiler_params=limit(6),
        name="embed",
    )(chooser(block_size), weight, embed_bias.reshape(1, emb), *parts)


def solution(mesh):
    placed = (
        P(None, ("groups", "dom")),
        P("dom", None, None),
        P("dom"),
        P("dom"),
        P("dom"),
        P("dom"),
        P(),
        P(),
    )
    return jax.shard_map(
        local,
        mesh=mesh,
        in_specs=placed,
        out_specs=(P(("groups", "dom"), None, None), P(("groups", "dom"), None)),
        check_vma=False,
    )
```
